128 devices in a mesh: tile: 8 (over z, core), seq: 16 (over x, y).
Axes of the slice: x: 4, y: 4, z: 4, core: 2. Of those that a mesh axis runs over, the one named last changes fastest.
Arguments:
- tile_feats: bfloat16 [65536, 1536], P(('tile', 'seq')), may hold values from -8 to 8
- tile_gain: float32 [1536], replicated, may hold values from 0.5 to 1.5
- proj_weight: bfloat16 [1536, 768], replicated, may hold values from -1 to 1
- proj_bias: float32 [768], replicated, may hold values from -3 to 3
- dest: int32 [65536, 1], P(('tile', 'seq')), may hold values from 0 to 127; in each aligned block of 512 rows (0 to 511, 512 to 1023, ...) at most 8 rows name the same one
- slot_gain: float32 [768], replicated, may hold values from 0.5 to 1.5
- qkv_weight: bfloat16 [768, 2304], replicated, may hold values from -1 to 1
- out_weight: bfloat16 [768, 768], replicated, may hold values from -0.21875 to 0.21875
- mlp_gain: float32 [768], replicated, may hold values from 0.5 to 1.5
- up_weight: bfloat16 [768, 3072], replicated, may hold values from -0.21875 to 0.21875
- down_weight: bfloat16 [3072, 768], replicated, may hold values from -0.109375 to 0.109375
- offsets: int32 [16], replicated, may hold values from 0 to 7, as said below
- slot_grad: bfloat16 [8, 16384, 768], P('tile', 'seq'), may hold values from -6 to 6
Outputs:
- slide_states: bfloat16 [8, 16384, 768], P('tile', 'seq')
- tile_grad: bfloat16 [65536, 1536], P(('tile', 'seq'))
The draws below stay inside these ranges and needn't reach their ends.
Inputs may be any that keep to these rules, and one draw needn't show every extreme that they name: `dest`: at most 8 of the rows of one device name the same owner; some owner receives exactly 8 from some device. `offsets`: the offset of head h is below 2 ** (h // 4).
All inputs are finite; a program needn't handle non-finite values.
Results may differ from the reference program's by a relative error of at most 0.0075.
Values may be sent and summed in bfloat16 or wider, within the bound.
No kernel may reach another device: no remote copies, remote signals or barrier semaphores. Data moves between devices by JAX's collectives and lax.ppermute only.
A program may use at most 192 MiB of HBM per device.

```python
import math
import jax
import jax.numpy as jnp
import numpy as np
from jax import lax

DT = 1536
D = 768
HEADS = 16
FF = 3072
HD = 48
TILE_DEV = 512
CAP = 8
SLOT_DEV = 1024
TILES = 65536
SLIDES = 8
L = 16384
N_SEQ = 16
DEVICES = 128


def draw_tile_feats(key, part):
    key = jax.random.fold_in(key, 11)
    noise_key = jax.random.fold_in(key, 0)
    noise = jax.random.normal(noise_key, (TILES, DT), jnp.float32)
    values = jnp.clip(noise, -6.0, 6.0)
    return values.astype(jnp.bfloat16)


def draw_proj_weight(key, part):
    key = jax.random.fold_in(key, 12)
    limit = 6.0 * DT ** (-0.5)
    base = jnp.clip(jax.random.normal(key, (DT, D), jnp.float32) * DT ** (-0.5), -limit, limit)
    values = base
    return jnp.clip(values, -1.0, 1.0).astype(jnp.bfloat16)


def draw_qkv_weight(key, part):
    key = jax.random.fold_in(key, 13)
    limit = 6.0 * D ** (-0.5)
    base = jnp.clip(jax.random.normal(key, (D, 3 * D), jnp.float32) * D ** (-0.5), -limit, limit)
    values = base
    return jnp.clip(values, -1.0, 1.0).astype(jnp.bfloat16)


def draw_offsets(key, part):
    key = jax.random.fold_in(key, 7)
    first, second = jax.random.split(key, 2)
    scores = jax.random.randint(first, (4, 4), 0, 1 << 20) * 4 + jnp.arange(4, dtype=jnp.int32)[None, :]
    ranks = jnp.argsort(scores, axis=1, stable=True).astype(jnp.int32)
    stride = (2 ** jnp.arange(4, dtype=jnp.int32))[:, None]
    extra = jax.random.randint(second, (4, 4), 0, jnp.maximum(stride // 4, 1))
    offset = ranks * stride // 4 + extra
    offset = jnp.where(ranks == 3, stride - 1, offset)
    return offset.reshape(HEADS).astype(jnp.int32)


def level_of(stream_key, shape, cuts, smallest, top_value):
    def one(axis_at, parts):
        heights = jax.random.uniform(jax.random.fold_in(jax.random.fold_in(stream_key, 6), axis_at), (parts,), jnp.float32, smallest / len(cuts), top_value / len(cuts))
        return jnp.repeat(jnp.exp(heights), shape[axis_at] // parts).reshape((-1,) + (1,) * (len(shape) - axis_at - 1))

    loudness = one(*cuts[0])
    for cut in cuts[1:]:
        loudness = loudness * one(*cut)
    return loudness


def shared_out(key, own, number, rows, amount, top, reach, lean):
    order = jax.random.permutation(key, amount)
    heavy_load, common = portions_of(amount, rows * top, reach, lean, True), portions_of(amount, rows * top, reach, lean, False)
    places = jnp.arange(amount)

    def named(tallies, rotation):
        used = int((tallies > 0).sum())
        fixed = max(1, used // 4)
        shifted = fixed + (places - fixed + rotation * (used - fixed)) % max(1, amount - fixed)
        return jnp.zeros((amount,), jnp.int32).at[order[jnp.where(places < fixed, places, shifted)]].set(jnp.asarray(tallies, jnp.int32))

    tallies = jnp.where(number % 4 == 0, named(heavy_load, number // 4), named(common, number - number // 4 - 1))
    mixed = jax.random.permutation(jax.random.fold_in(own, 3), amount)
    donor, sink = mixed[0:amount // 2 * 2:2], mixed[1:amount // 2 * 2:2]
    room = jnp.minimum(tallies[donor] - 1, reach - tallies[sink]) // 2
    room = jnp.where((donor == order[0]) | (sink == order[0]) | (tallies[sink] == 0), 0, jnp.maximum(room, 0))
    shifted = jax.random.randint(jax.random.fold_in(own, 4), (amount // 2,), 0, 1 << 20) % (room + 1)
    tallies = tallies.at[donor].add(-shifted).at[sink].add(shifted)
    members = jnp.searchsorted(jnp.cumsum(tallies), jnp.arange(rows * top), side="right").astype(jnp.int32)
    table = members.reshape(top, rows).T
    table = table[jax.random.permutation(jax.random.fold_in(own, 1), rows)]
    rotation = jax.random.randint(jax.random.fold_in(own, 2), (rows, 1), 0, top)
    return jnp.take_along_axis(table, (jnp.arange(top)[None, :] + rotation) % top, axis=1)


def portions_of(number_of, total, most, slope, full):
    loads = [(1 << 20) // math.isqrt(standing ** slope) + 1 for standing in range(1, number_of + 1)]
    largest = most if full else min(most, max(-(-total // number_of), total * loads[0] // sum(loads)))
    least = 1 if total - largest >= number_of - 1 else 0
    given, rest = [largest] + [least] * (number_of - 1), total - largest - least * (number_of - 1)
    while rest > 0:
        free = [i for i in range(1, number_of) if given[i] < largest] or [i for i in range(1, number_of) if given[i] < most]
        whole, budget = sum([loads[i] for i in free]), rest
        for i in free:
            addition = min(most - given[i], max(1, budget * loads[i] // whole), rest)
            given[i] = given[i] + addition
            rest = rest - addition
    return np.array(given)


def normal_values(key, extent, width, bound, cuts=(), held_as=jnp.bfloat16):
    values = width * jax.random.normal(key, extent, jnp.float32)
    if cuts:
        values = values * level_of(key, extent, cuts, -0.22, 0.18)
    return jnp.clip(values, -bound, bound).astype(held_as)


def setup_inputs(seed: int = 0) -> dict:
    seeds = jax.random.split(jax.random.key(seed), 14)
    tile_feats = draw_tile_feats(jax.random.fold_in(seeds[13], 71), 0)
    tile_gain = jnp.clip(1.0 + 0.1 * jax.random.normal(seeds[1], (DT,), jnp.float32), 0.5, 1.5)
    proj_weight = draw_proj_weight(jax.random.fold_in(seeds[13], 71), 0)
    proj_bias = normal_values(seeds[3], (D,), 0.5, 3.0, (), jnp.float32)
    dest_keys = jax.random.split(jax.random.fold_in(seeds[4], 1), TILES // TILE_DEV)
    dest_turns = jax.random.permutation(jax.random.fold_in(seeds[4], 3), TILES // TILE_DEV)
    dest = jax.vmap(lambda own, number: shared_out(jax.random.fold_in(seeds[4], 2), own, number, TILE_DEV, DEVICES, 1, CAP, 2))(dest_keys, dest_turns).reshape((TILES, 1))
    slot_gain = jnp.clip(1.0 + 0.1 * jax.random.normal(seeds[5], (D,), jnp.float32), 0.5, 1.5)
    qkv_weight = draw_qkv_weight(jax.random.fold_in(seeds[13], 71), 0)
    out_weight = normal_values(seeds[7], (D, D), D ** -0.5, 0.21875)
    mlp_gain = jnp.clip(1.0 + 0.1 * jax.random.normal(seeds[8], (D,), jnp.float32), 0.5, 1.5)
    up_weight = normal_values(seeds[9], (D, FF), D ** -0.5, 0.21875)
    down_weight = normal_values(seeds[10], (FF, D), FF ** -0.5, 0.109375)
    offsets = draw_offsets(jax.random.fold_in(seeds[13], 71), 0)
    slot_grad = normal_values(seeds[12], (SLIDES, L, D), 1.0, 6.0, ((0, 8), (1, 16)))
    return {"tile_feats": tile_feats, "tile_gain": tile_gain, "proj_weight": proj_weight, "proj_bias": proj_bias, "dest": dest, "slot_gain": slot_gain, "qkv_weight": qkv_weight, "out_weight": out_weight, "mlp_gain": mlp_gain, "up_weight": up_weight, "down_weight": down_weight, "offsets": offsets, "slot_grad": slot_grad}


eps = 1e-05

def norm_rows(values, gain):
    mean = lax.optimization_barrier(jnp.mean(values, axis=-1, keepdims=True))
    centred = values - mean
    spread = lax.optimization_barrier(jnp.mean(centred * centred, axis=-1, keepdims=True))
    return centred * lax.rsqrt(spread + eps) * gain

def slot_layout(dest):
    target = dest[:, 0].reshape(DEVICES, TILE_DEV)
    owners = jnp.arange(DEVICES, dtype=jnp.int32)
    onehot = (target[:, :, None] == owners[None, None, :]).astype(jnp.int32)
    before = jnp.cumsum(onehot, axis=1) - onehot
    rank = lax.optimization_barrier(jnp.sum(before * onehot, axis=2))
    source = owners[:, None]
    position = target % N_SEQ * SLOT_DEV + source * CAP + rank
    slide = target // N_SEQ
    return (slide.reshape(-1).astype(jnp.int32), position.reshape(-1).astype(jnp.int32))

def longnet(slide_in, valid, slot_gain, qkv_weight, out_weight, mlp_gain, up_weight, down_weight, offsets):
    residual = slide_in.astype(jnp.float32)
    normed = norm_rows(residual, slot_gain).astype(jnp.bfloat16)
    mixed = jnp.dot(normed, qkv_weight, preferred_element_type=jnp.float32).astype(jnp.bfloat16)
    query = mixed[:, :D]
    key = mixed[:, D:2 * D]
    value = mixed[:, 2 * D:]
    heads = []
    for head in range(HEADS):
        group = head // (HEADS // 4)
        stride = 2 ** group
        span = L // 2 ** (3 - group)
        offset = offsets[head]

        def pick(array):
            shaped = array.reshape((L // span, span // stride, stride) + array.shape[1:])
            return jnp.take(shaped, offset, axis=2)
        lo = head * HD
        q_sel = pick(query[:, lo:lo + HD]).astype(jnp.float32)
        k_sel = pick(key[:, lo:lo + HD]).astype(jnp.float32)
        v_sel = pick(value[:, lo:lo + HD]).astype(jnp.float32)
        k_ok = pick(valid)
        scores = jnp.einsum('sqd,skd->sqk', q_sel, k_sel) * HD ** (-0.5)
        scores = jnp.where(k_ok[:, None, :] > 0, scores, -1e+30)
        top = lax.optimization_barrier(jnp.max(scores, axis=2, keepdims=True))
        weights = jnp.exp(scores - top)
        probs = (weights / lax.optimization_barrier(jnp.sum(weights, axis=2, keepdims=True))).astype(jnp.bfloat16)
        result = jnp.einsum('sqk,skd->sqd', probs.astype(jnp.float32), v_sel)
        chosen = (jnp.arange(stride, dtype=jnp.int32) == offset).astype(jnp.float32)
        placed = result[:, :, None, :] * chosen[None, None, :, None]
        heads.append(placed.reshape(L, HD))
    attn = jnp.concatenate(heads, axis=1).astype(jnp.bfloat16)
    hidden = residual + jnp.dot(attn, out_weight, preferred_element_type=jnp.float32)
    mlp_normed = norm_rows(hidden, mlp_gain).astype(jnp.bfloat16)
    act = jax.nn.gelu(jnp.dot(mlp_normed, up_weight, preferred_element_type=jnp.float32)).astype(jnp.bfloat16)
    final = hidden + jnp.dot(act, down_weight, preferred_element_type=jnp.float32)
    return jnp.where(valid[:, None] > 0, final, 0.0).astype(jnp.bfloat16)

def reference(tile_feats, tile_gain, proj_weight, proj_bias, dest, slot_gain, qkv_weight, out_weight, mlp_gain, up_weight, down_weight, offsets, slot_grad):
    feats = tile_feats.astype(jnp.float32)
    tile_normed = norm_rows(feats, tile_gain).astype(jnp.bfloat16)
    emb = (jnp.dot(tile_normed, proj_weight, preferred_element_type=jnp.float32) + proj_bias).astype(jnp.bfloat16)
    slide, position = slot_layout(dest)
    slide_in = jnp.zeros((SLIDES, L, D), jnp.bfloat16).at[slide, position].set(emb)
    valid = jnp.zeros((SLIDES, L), jnp.int32).at[slide, position].set(1)

    def one_slide(pair):
        return longnet(pair[0], pair[1], slot_gain, qkv_weight, out_weight, mlp_gain, up_weight, down_weight, offsets)
    slide_states = lax.map(one_slide, (slide_in, valid))
    grad_rows = slot_grad[slide, position]
    normed_grad = lax.dot_general(grad_rows, proj_weight, (((1,), (1,)), ((), ())), preferred_element_type=jnp.float32)
    unused, pullback = jax.vjp(lambda values: norm_rows(values, tile_gain), feats)
    tile_grad = pullback(normed_grad)[0].astype(jnp.bfloat16)
    return (slide_states, tile_grad)
```

```python
import math

import jax
import jax.numpy as jnp
from jax import lax
from jax.experimental import pallas as pl
from jax.experimental.pallas import tpu as pltpu
from jax.sharding import PartitionSpec as P

DT = 1536
D = 768
HEADS = 16
FF = 3072
HD = 48
TILES = 512
CAP = 8
OWNERS = 128
SLOTS = 1024
KEYS = 2048
N_SEQ = 16
EPS = 1e-05
MIB = 2**20

EMPTY = 3e38
LIMIT = 1e37
MASKED = -1e30
SCALE = HD**-0.5 * math.log2(math.e)

BF = jnp.bfloat16
F32 = jnp.float32
NT = (((1,), (1,)), ((), ()))
TN = (((0,), (0,)), ((), ()))


def iota(shape, axis):
    return lax.broadcasted_iota(jnp.int32, shape, axis)


def normalise(values):
    mean = jnp.mean(values, axis=-1, keepdims=True)
    centred = values - mean
    spread = jnp.mean(centred * centred, axis=-1, keepdims=True)
    return centred, lax.rsqrt(spread + EPS)


def call(kernel, outs, scratch, vmem, flops, name, in_specs=None):
    specs = {} if in_specs is None else {"in_specs": in_specs}
    return pl.pallas_call(
        kernel,
        out_shape=outs,
        **specs,
        scratch_shapes=scratch,
        name=name,
        compiler_params=pltpu.CompilerParams(vmem_limit_bytes=vmem * MIB),
        cost_estimate=pl.CostEstimate(flops=flops, bytes_accessed=8 * MIB, transcendentals=0),
    )


VM = pl.BlockSpec(memory_space=pltpu.VMEM)
SM = pl.BlockSpec(memory_space=pltpu.SMEM)


def embed_kernel(dest_ref, feats_ref, gain_ref, weight_ref, bias_ref, out_ref):
    centred, scale = normalise(feats_ref[...].astype(F32))
    normed = (centred * scale * gain_ref[...]).astype(BF)
    emb = jnp.dot(normed, weight_ref[...], preferred_element_type=F32) + bias_ref[...]
    emb = emb.astype(BF)
    dest = dest_ref[...]
    hot = (iota((OWNERS, TILES), 0) == dest).astype(F32)
    earlier = (iota((TILES, TILES), 0) < iota((TILES, TILES), 1)).astype(F32).astype(BF)
    before = jnp.dot(hot.astype(BF), earlier, preferred_element_type=F32)
    rank = jnp.sum(before * hot, axis=0, keepdims=True).astype(jnp.int32)
    place = (iota((SLOTS, TILES), 0) == dest * CAP + rank).astype(F32)
    taken = jnp.max(place, axis=1, keepdims=True)
    rows = jnp.dot(place.astype(BF), emb, preferred_element_type=F32)
    out_ref[...] = jnp.where(taken > 0, rows, EMPTY).astype(BF)


def qkv_kernel(
    off_ref,
    slots_ref,
    gain_ref,
    weight_ref,
    rows_ref,
    q0_ref,
    kv0_ref,
    s1_ref,
    s2_ref,
    s3_ref,
    wide,
    normed,
    mixed,
):
    for c in range(D // 128):
        wide[c] = slots_ref[:, c * 128 : (c + 1) * 128].astype(F32)
    flags = []
    for r in range(CAP):
        rows = jnp.concatenate(
            [wide[c, pl.ds(r, OWNERS, stride=CAP), :] for c in range(D // 128)], axis=1
        )
        rows_ref[r * OWNERS : (r + 1) * OWNERS, :] = rows.astype(BF)
        held = rows[:, :1] < LIMIT
        flags.append(jnp.broadcast_to(held.astype(F32), (OWNERS, 128)).T[:1])
        centred, scale = normalise(jnp.where(held, rows, 0.0))
        normed[r * OWNERS : (r + 1) * OWNERS, :] = (centred * scale * gain_ref[...]).astype(BF)
    held = jnp.concatenate(flags, axis=1) > 0
    for part in range(3):
        rows = pl.ds(part * D, D)
        block = lax.dot_general(
            weight_ref[rows, :], normed[...], NT, preferred_element_type=F32
        )
        if part == 0:
            block = block * SCALE
        if part == 1:
            block = jnp.where(held, block, EMPTY)
        mixed[rows, :] = block.astype(BF)

    def piece(part, head, rank):
        lanes = pl.ds(pl.multiple_of(rank * OWNERS, OWNERS), OWNERS)
        return mixed[part * D + head * HD : part * D + (head + 1) * HD, lanes]

    q0_ref[...] = mixed[0 : 4 * HD, :]
    kv0_ref[0 : 4 * HD, :] = mixed[D : D + 4 * HD, :]
    kv0_ref[4 * HD :, :] = mixed[2 * D : 2 * D + 4 * HD, :]
    for j in range(4):
        for part in range(3):
            for i in range(4):
                s1_ref[j, part * HD : (part + 1) * HD, i * 128 : (i + 1) * 128] = piece(
                    part, 4 + j, off_ref[4 + j] + 2 * i
                )
    for j in range(8):
        head = 8 + j // 2
        off = off_ref[head]
        for i in range(2):
            s2_ref[j, i * HD : (i + 1) * HD, :] = piece(1, head, off + 4 * i)
            s2_ref[j, (2 + i) * HD : (3 + i) * HD, :] = piece(2, head, off + 4 * i)
        s2_ref[j, 4 * HD : 5 * HD, :] = piece(0, head, off + 4 * (j % 2))
    for j in range(16):
        head = 12 + j // 4
        for part in range(3):
            s3_ref[j, part * HD : (part + 1) * HD, :] = piece(part, head, off_ref[head])


def finish_keys(keys, values):
    top = iota((16, KEYS), 0) == 0
    empty = keys[0:1, :].astype(F32) > LIMIT
    keys[HD:, :] = jnp.where(top & empty, MASKED, 0.0).astype(BF)
    keys[:HD, :] = jnp.where(empty, 0.0, keys[:HD, :].astype(F32)).astype(BF)
    values[HD:, :] = jnp.where(top, 1.0, 0.0).astype(BF)


def with_ones(query):
    width = query.shape[1]
    ones = jnp.where(iota((16, width), 0) == 0, 1.0, 0.0).astype(BF)
    return jnp.concatenate([query, ones], axis=0)


def attend(query, keys, values):
    scores = jnp.dot(keys, query, preferred_element_type=F32)
    top = jnp.max(scores, axis=0, keepdims=True)
    weights = jnp.exp2(scores - top).astype(BF)
    result = jnp.dot(values, weights, preferred_element_type=F32)
    return (result[:HD] / jnp.maximum(result[HD : HD + 1], 1e-30)).astype(BF)


def attend0_kernel(q_ref, own_ref, other_ref, out_ref, keys, values):
    def one(head, carry):
        rows = pl.ds(pl.multiple_of(head * HD, 16), HD)
        vrows = pl.ds(pl.multiple_of((4 + head) * HD, 16), HD)
        keys[:HD, :SLOTS] = own_ref[rows, :]
        keys[:HD, SLOTS:] = other_ref[rows, :]
        values[:HD, :SLOTS] = own_ref[vrows, :]
        values[:HD, SLOTS:] = other_ref[vrows, :]
        finish_keys(keys, values)
        turned = keys[...].T
        for t in range(2):
            lanes = slice(t * 512, (t + 1) * 512)
            out_ref[rows, lanes] = attend(with_ones(q_ref[rows, lanes]), turned, values[...])
        return carry

    lax.fori_loop(0, 4, one, 0)


def attend1_kernel(got_ref, out_ref, keys, values):
    for s in range(4):
        lanes = slice(s * 512, (s + 1) * 512)
        keys[:HD, lanes] = got_ref[s, HD : 2 * HD, :]
        values[:HD, lanes] = got_ref[s, 2 * HD : 3 * HD, :]
    finish_keys(keys, values)
    turned = keys[...].T

    def one(s, carry):
        out_ref[s] = attend(with_ones(got_ref[s, :HD, :]), turned, values[...])
        return carry

    lax.fori_loop(0, 4, one, 0)


def attend2_kernel(got_ref, out_ref, keys, values):
    for s in range(8):
        for i in range(2):
            lanes = slice((2 * s + i) * 128, (2 * s + i + 1) * 128)
            keys[:HD, lanes] = got_ref[s, i * HD : (i + 1) * HD, :]
            values[:HD, lanes] = got_ref[s, (2 + i) * HD : (3 + i) * HD, :]
    finish_keys(keys, values)
    turned = keys[...].T
    for t in range(2):
        query = jnp.concatenate([got_ref[4 * t + s, 4 * HD :, :] for s in range(4)], axis=1)
        result = attend(with_ones(query), turned, values[...])
        for s in range(4):
            out_ref[4 * t + s] = result[:, s * 128 : (s + 1) * 128]


def attend3_kernel(me_ref, got_ref, two_ref, out_ref, keys, values, pick):
    for s in range(N_SEQ):
        lanes = slice(s * 128, (s + 1) * 128)
        keys[:HD, lanes] = got_ref[s, HD : 2 * HD, :]
        values[:HD, lanes] = got_ref[s, 2 * HD : 3 * HD, :]
    finish_keys(keys, values)
    at = iota((KEYS, 512), 0)
    lane = at % 128 - (me_ref[0] % 4) * 32
    wanted = jnp.where((lane >= 0) & (lane < 32), at // 128 * 32 + lane, -1)
    pick[...] = (wanted == iota((KEYS, 512), 1)).astype(F32).astype(BF)
    queries = jnp.concatenate([got_ref[s, :HD, :] for s in range(N_SEQ)], axis=1)
    query = jnp.dot(queries, pick[...], preferred_element_type=F32).astype(BF)
    result = attend(with_ones(query), keys[...].T, values[...])
    spread = lax.dot_general(result, pick[...], NT, preferred_element_type=F32).astype(BF)
    base = me_ref[0] // 8 * 8
    out_ref[:, :HD, :] = jnp.zeros((N_SEQ, HD, 128), BF)
    out_ref[pl.ds(base, 8), :HD, :] = two_ref[...]
    for s in range(N_SEQ):
        out_ref[s, HD:, :] = spread[:, s * 128 : (s + 1) * 128]


def mlp_kernel(
    off_ref,
    me_ref,
    rows_ref,
    a0_ref,
    a1_ref,
    a23_ref,
    gain_ref,
    out_weight_ref,
    up_ref,
    down_ref,
    out_ref,
    attn,
    wide,
):
    attn[: 4 * HD, :] = a0_ref[...]
    attn[4 * HD :, :] = jnp.zeros((12 * HD, SLOTS), BF)

    def lanes(rank):
        return pl.ds(pl.multiple_of(rank * OWNERS, OWNERS), OWNERS)

    for j in range(4):
        head = 4 + j
        for i in range(4):
            attn[head * HD : (head + 1) * HD, lanes(off_ref[head] + 2 * i)] = a1_ref[
                j, :, i * 128 : (i + 1) * 128
            ]
    base = me_ref[0] // 8 * 8
    for j in range(8):
        head = 8 + j // 2
        attn[head * HD : (head + 1) * HD, lanes(off_ref[head] + 4 * (j % 2))] = a23_ref[
            base + j, :HD, :
        ]
    for j in range(4):
        head = 12 + j
        total = a23_ref[4 * j, HD:, :].astype(F32)
        for k in range(1, 4):
            total = total + a23_ref[4 * j + k, HD:, :].astype(F32)
        attn[head * HD : (head + 1) * HD, lanes(off_ref[head])] = total.astype(BF)

    tile = 256
    for t in range(SLOTS // tile):
        span = slice(t * tile, (t + 1) * tile)
        rows = rows_ref[span, :].astype(F32)
        held = rows[:, :1] < LIMIT
        hidden = jnp.where(held, rows, 0.0) + lax.dot_general(
            attn[:, span], out_weight_ref[...], TN, preferred_element_type=F32
        )
        centred, scale = normalise(hidden)
        normed = (centred * scale * gain_ref[...]).astype(BF)
        final = hidden
        for f in range(4):
            cols = slice(f * 768, (f + 1) * 768)
            act = jnp.dot(normed, up_ref[:, cols], preferred_element_type=F32)
            act = jax.nn.gelu(act).astype(BF)
            final = final + jnp.dot(act, down_ref[cols, :], preferred_element_type=F32)
        final = jnp.where(held, final, 0.0)
        for i in range(tile // OWNERS):
            r = t * (tile // OWNERS) + i
            for c in range(D // 128):
                wide[c, pl.ds(r, OWNERS, stride=CAP), :] = final[
                    i * OWNERS : (i + 1) * OWNERS, c * 128 : (c + 1) * 128
                ]
    for c in range(D // 128):
        out_ref[0, :, c * 128 : (c + 1) * 128] = wide[c].astype(BF)


def grad_kernel(dest_ref, feats_ref, gain_ref, weight_ref, back_ref, out_ref):
    dest = dest_ref[...]
    hot = (iota((TILES, OWNERS), 1) == dest).astype(F32)
    earlier = (iota((TILES, TILES), 1) < iota((TILES, TILES), 0)).astype(F32).astype(BF)
    before = jnp.dot(earlier, hot.astype(BF), preferred_element_type=F32)
    rank = jnp.sum(before * hot, axis=1, keepdims=True).astype(jnp.int32)
    place = (iota((TILES, SLOTS), 1) == dest * CAP + rank).astype(F32).astype(BF)
    rows = jnp.dot(place, back_ref[...], preferred_element_type=F32).astype(BF)
    grad = lax.dot_general(rows, weight_ref[...], NT, preferred_element_type=F32)
    grad = grad * gain_ref[...]
    centred, scale = normalise(feats_ref[...].astype(F32))
    unit = centred * scale
    along = jnp.mean(grad * unit, axis=-1, keepdims=True)
    level = jnp.mean(grad, axis=-1, keepdims=True)
    out_ref[...] = (scale * (grad - level - unit * along)).astype(BF)


def per_device(
    tile_feats,
    tile_gain,
    proj_weight,
    proj_bias,
    dest,
    slot_gain,
    qkv_weight,
    out_weight,
    mlp_gain,
    up_weight,
    down_weight,
    offsets,
    slot_grad,
):
    sds = jax.ShapeDtypeStruct
    everyone = ("tile", "seq")
    me = lax.axis_index("seq").astype(jnp.int32).reshape(1)
    tile_gain = tile_gain.reshape(1, DT)

    def groups(size):
        return [list(range(b, b + size)) for b in range(0, N_SEQ, size)]

    def swap(array, size):
        return lax.all_to_all(
            array, "seq", split_axis=0, concat_axis=0, tiled=True, axis_index_groups=groups(size)
        )

    outgoing = call(
        embed_kernel, sds((SLOTS, D), BF), (), 40, 2 * 10**9, "embed_tiles"
    )(dest.reshape(1, TILES), tile_feats, tile_gain, proj_weight, proj_bias.reshape(1, D))
    slots = lax.all_to_all(outgoing, everyone, split_axis=0, concat_axis=0, tiled=True)

    rows, q0, kv0, s1, s2, s3 = call(
        qkv_kernel,
        (
            sds((SLOTS, D), BF),
            sds((4 * HD, SLOTS), BF),
            sds((8 * HD, SLOTS), BF),
            sds((4, 3 * HD, 512), BF),
            sds((8, 5 * HD, 128), BF),
            sds((16, 3 * HD, 128), BF),
        ),
        (pltpu.VMEM((D // 128, SLOTS, 128), F32), pltpu.VMEM((SLOTS, D), BF), pltpu.VMEM((3 * D, SLOTS), BF)),
        48,
        4 * 10**9,
        "make_qkv",
        [SM, VM, VM, VM],
    )(offsets, slots, slot_gain.reshape(1, D), qkv_weight.T)

    pair = [(i, i ^ 1) for i in range(N_SEQ)]
    kv0_other = lax.ppermute(kv0, "seq", pair)
    got3 = swap(s3, 16)
    got2 = swap(s2, 8)
    got1 = swap(s1, 4)

    key_scratch = (pltpu.VMEM((64, KEYS), BF), pltpu.VMEM((64, KEYS), BF))
    o3_in = got3
    o2 = call(
        attend2_kernel, sds((8, HD, 128), BF), key_scratch, 40, 4 * 10**9, "attend_group2"
    )(got2)
    s23 = call(
        attend3_kernel,
        sds((N_SEQ, 2 * HD, 128), BF),
        key_scratch + (pltpu.VMEM((KEYS, 512), BF),),
        40,
        2 * 10**9,
        "attend_group3",
        [SM, VM, VM],
    )(me, o3_in, o2)
    o1 = call(
        attend1_kernel, sds((4, HD, 512), BF), key_scratch, 40, 8 * 10**9, "attend_group1"
    )(got1)
    back23 = swap(s23, 16)
    back1 = swap(o1, 4)
    a0 = call(
        attend0_kernel, sds((4 * HD, SLOTS), BF), key_scratch, 40, 16 * 10**9, "attend_group0"
    )(q0, kv0, kv0_other)

    slide_states = call(
        mlp_kernel,
        sds((1, SLOTS, D), BF),
        (pltpu.VMEM((D, SLOTS), BF), pltpu.VMEM((D // 128, SLOTS, 128), F32)),
        56,
        11 * 10**9,
        "out_and_mlp",
        [SM, SM] + [VM] * 8,
    )(
        offsets,
        me,
        rows,
        a0,
        back1,
        back23,
        mlp_gain.reshape(1, D),
        out_weight,
        up_weight,
        down_weight,
    )

    returned = lax.all_to_all(slot_grad[0], everyone, split_axis=0, concat_axis=0, tiled=True)
    tile_grad = call(
        grad_kernel, sds((TILES, DT), BF), (), 40, 2 * 10**9, "tile_cotangent"
    )(dest, tile_feats, tile_gain, proj_weight, returned)
    return (slide_states, tile_grad)


def solution(mesh):
    return jax.shard_map(
        per_device,
        mesh=mesh,
        in_specs=(
            P(("tile", "seq"), None),
            P(),
            P(),
            P(),
            P(("tile", "seq"), None),
            P(),
            P(),
            P(),
            P(),
            P(),
            P(),
            P(),
            P("tile", "seq", None),
        ),
        out_specs=(P("tile", "seq", None), P(("tile", "seq"), None)),
        check_vma=False,
    )
```

```python
import math

import jax
import jax.numpy as jnp
from jax import lax
from jax.experimental import pallas as pl
from jax.experimental.pallas import tpu as pltpu
from jax.sharding import PartitionSpec as P

DT = 1536
D = 768
HEADS = 16
FF = 3072
HD = 48
TILES = 512
CAP = 8
OWNERS = 128
SLOTS = 1024
KEYS = 2048
N_SEQ = 16
EPS = 1e-05
MIB = 2**20
VMEM = 32

EMPTY = 3e38
LIMIT = 1e37
MASKED = -1e30
SCALE = HD**-0.5 * math.log2(math.e)

BF = jnp.bfloat16
F32 = jnp.float32
NT = (((1,), (1,)), ((), ()))
TN = (((0,), (0,)), ((), ()))


def iota(shape, axis):
    return lax.broadcasted_iota(jnp.int32, shape, axis)


def normalise(values):
    mean = jnp.mean(values, axis=-1, keepdims=True)
    centred = values - mean
    spread = jnp.mean(centred * centred, axis=-1, keepdims=True)
    return centred, lax.rsqrt(spread + EPS)


def call(kernel, outs, scratch, vmem, flops, name, in_specs=None, out_specs=None):
    specs = {} if in_specs is None else {"in_specs": in_specs}
    if out_specs is not None:
        specs["out_specs"] = out_specs
    return pl.pallas_call(
        kernel,
        out_shape=outs,
        **specs,
        scratch_shapes=scratch,
        name=name,
        compiler_params=pltpu.CompilerParams(vmem_limit_bytes=vmem * MIB),
        cost_estimate=pl.CostEstimate(flops=flops, bytes_accessed=8 * MIB, transcendentals=0),
    )


VM = pl.BlockSpec(memory_space=pltpu.VMEM)
SM = pl.BlockSpec(memory_space=pltpu.SMEM)
HBM = pl.BlockSpec(memory_space=pltpu.HBM)
DMA = pltpu.SemaphoreType.DMA


def started(copies):
    for copy in copies:
        copy.start()
    return copies


def finish(copies):
    for copy in copies:
        copy.wait()


GROUPS = ((1, 0, 4), (2, 512, 2), (3, 768, 1))
TAKEN = 896


def row_of(ref):
    return ref[...].reshape(1, ref.shape[0])


def rank_of(dest):
    hot = (iota((OWNERS, TILES), 0) == dest).astype(F32)
    earlier = (iota((TILES, TILES), 0) < iota((TILES, TILES), 1)).astype(F32).astype(BF)
    before = jnp.dot(hot.astype(BF), earlier, preferred_element_type=F32)
    return jnp.sum(before * hot, axis=0, keepdims=True).astype(jnp.int32)


def embed_kernel(
    dest_ref, feats_hbm, gain_ref, weight_hbm, bias_ref, out_hbm, feats, weight, out, sems
):
    loads = started(
        [
            pltpu.make_async_copy(feats_hbm, feats, sems.at[0]),
            pltpu.make_async_copy(weight_hbm, weight, sems.at[1]),
        ]
    )
    dest = dest_ref[...]
    place = (iota((SLOTS, TILES), 0) == dest * CAP + rank_of(dest)).astype(F32)
    taken = jnp.max(place, axis=1, keepdims=True)
    loads[0].wait()
    centred, scale = normalise(feats[...].astype(F32))
    normed = (centred * scale * row_of(gain_ref)).astype(BF)
    loads[1].wait()
    emb = jnp.dot(normed, weight[...], preferred_element_type=F32) + row_of(bias_ref)
    rows = jnp.dot(place.astype(BF), emb.astype(BF), preferred_element_type=F32)
    out[...] = jnp.where(taken > 0, rows, EMPTY).astype(BF)
    finish(started([pltpu.make_async_copy(out, out_hbm, sems.at[2])]))


def turn_kernel(weight_ref, out_ref):
    for i in range(6):
        cols = slice(i * 384, (i + 1) * 384)
        out_ref[cols, :] = weight_ref[:, cols].T


def qkv_kernel(
    off_ref,
    me_ref,
    slots_ref,
    gain_ref,
    weight_hbm,
    q0_ref,
    kv0_ref,
    sa_ref,
    sb_hbm,
    sc_hbm,
    sd_hbm,
    kv0_hbm,
    wide,
    mixed,
    weight,
    sent,
    sems,
):
    loads = started([pltpu.make_async_copy(weight_hbm, weight, sems.at[0])])
    for c in range(D // 128):
        wide[c] = slots_ref[:, c * 128 : (c + 1) * 128].astype(F32)
    gain = row_of(gain_ref)

    def prepared(block):
        flags, normed = [], []
        for r in (2 * block, 2 * block + 1):
            rows = jnp.concatenate(
                [wide[c, pl.ds(r, OWNERS, stride=CAP), :] for c in range(D // 128)], axis=1
            )
            held = rows[:, :1] < LIMIT
            flags.append(jnp.broadcast_to(held.astype(F32), (OWNERS, 128)).T[:1])
            centred, scale = normalise(jnp.where(held, rows, 0.0))
            normed.append((centred * scale * gain).astype(BF))
        return jnp.concatenate(flags, axis=1) > 0, jnp.concatenate(normed, axis=0)

    state = prepared(0)
    finish(loads)
    for block in range(4):
        held, normed = state
        if block < 3:
            state = prepared(block + 1)
        lanes = slice(block * 256, (block + 1) * 256)
        for part in range(3):
            rows = slice(part * D, (part + 1) * D)
            made = lax.dot_general(weight[rows, :], normed, NT, preferred_element_type=F32)
            if part == 0:
                made = made * SCALE
            if part == 1:
                made = jnp.where(held, made, EMPTY)
            mixed[rows, lanes] = made.astype(BF)
    copies = started(
        [
            pltpu.make_async_copy(mixed.at[pl.ds(D, 4 * HD)], kv0_hbm.at[pl.ds(0, 4 * HD)], sems.at[1]),
            pltpu.make_async_copy(
                mixed.at[pl.ds(2 * D, 4 * HD)], kv0_hbm.at[pl.ds(4 * HD, 4 * HD)], sems.at[2]
            ),
        ]
    )

    def piece(part, head, rank):
        lanes = pl.ds(pl.multiple_of(rank * OWNERS, OWNERS), OWNERS)
        return mixed[pl.ds(pl.multiple_of(part * D + head * HD, 16), HD), lanes]

    for m in (1, 2, 3, 0):
        ref = sent.at[m - 1] if m else sa_ref
        place = lax.bitwise_xor(me_ref[0] % 4, m)
        for group, start, count in GROUPS:
            head = 4 * group + place
            for row, part in enumerate((1, 2, 0)):
                for i in range(count):
                    ref[row * HD : (row + 1) * HD, start + i * 128 : start + (i + 1) * 128] = piece(
                        part, head, off_ref[head] + 2**group * i
                    )
        if m:
            target = (sb_hbm, sc_hbm, sd_hbm)[m - 1]
            copies += started([pltpu.make_async_copy(ref, target, sems.at[2 + m])])
    q0_ref[...] = mixed[0 : 4 * HD, :]
    kv0_ref[0 : 4 * HD, :] = mixed[D : D + 4 * HD, :]
    kv0_ref[4 * HD :, :] = mixed[2 * D : 2 * D + 4 * HD, :]
    finish(copies)


def finish_keys(keys, values):
    width = keys.shape[1]
    top = iota((16, width), 0) == 0
    empty = keys[0:1, :].astype(F32) > LIMIT
    keys[HD:, :] = jnp.where(top & empty, MASKED, 0.0).astype(BF)
    keys[:HD, :] = jnp.where(empty, 0.0, keys[:HD, :].astype(F32)).astype(BF)
    values[HD:, :] = jnp.where(top, 1.0, 0.0).astype(BF)


def with_ones(query):
    width = query.shape[1]
    ones = jnp.where(iota((16, width), 0) == 0, 1.0, 0.0).astype(BF)
    return jnp.concatenate([query, ones], axis=0)


def attend(units):
    def score(unit):
        return jnp.dot(with_ones(unit[0]()).T, unit[1](), preferred_element_type=F32)

    scores = score(units[0])
    for i, unit in enumerate(units):
        top = jnp.max(scores, axis=1, keepdims=True)
        later = score(units[i + 1]) if i + 1 < len(units) else None
        weights = jnp.exp2(scores - top).astype(BF)
        sums = lax.dot_general(weights, unit[2](), NT, preferred_element_type=F32)
        unit[3](sums, top)
        scores = later


def divided(sums):
    turned = sums.T
    return (turned[:HD] / jnp.maximum(turned[HD : HD + 1], 1e-30)).astype(BF)


QT = 256


def units0(q_ref, keys, values, done):
    units = []
    for head in range(4):
        for t in range(SLOTS // QT):
            rows, lanes = slice(head * HD, (head + 1) * HD), slice(t * QT, (t + 1) * QT)
            units.append(
                (
                    lambda rows=rows, lanes=lanes: q_ref[rows, lanes],
                    lambda head=head: keys[head],
                    lambda head=head: values[head],
                    lambda sums, top, at=(head, rows, lanes): done(sums, top, *at),
                )
            )
    return units


def load0(kv_ref, keys, values):
    for head in range(4):
        keys[head, :HD] = kv_ref[head * HD : (head + 1) * HD, :]
        values[head, :HD] = kv_ref[(4 + head) * HD : (5 + head) * HD, :]
        finish_keys(keys.at[head], values.at[head])


def own_half_kernel(q_ref, kv_ref, out_ref, keys, values):
    load0(kv_ref, keys, values)

    def done(sums, top, head, rows, lanes):
        turned = jnp.where(iota((QT, 64), 1) == HD + 1, top, sums).T
        out_ref[head, :, lanes] = turned

    attend(units0(q_ref, keys, values, done))


def other_half_kernel(q_ref, kv_ref, half_ref, out_ref, keys, values):
    load0(kv_ref, keys, values)

    def done(sums, top, head, rows, lanes):
        mine = jnp.where(iota((QT, 64), 1) == HD + 1, top, sums).T
        before = half_ref[head, :, lanes]
        top_mine, top_before = mine[HD + 1 : HD + 2], before[HD + 1 : HD + 2]
        top = jnp.maximum(top_mine, top_before)
        total = mine * jnp.exp2(top_mine - top) + before * jnp.exp2(top_before - top)
        out_ref[rows, lanes] = (total[:HD] / jnp.maximum(total[HD : HD + 1], 1e-30)).astype(BF)

    attend(units0(q_ref, keys, values, done))


def pack_kernel(*refs):
    got, (far_hbm, farther_hbm, far, sems) = refs[:4], refs[4:]
    for s in range(4):
        far[:, s * 256 : (s + 1) * 256] = got[s][: 2 * HD, 512:768]
        far[:, 1024 + s * 128 : 1024 + (s + 1) * 128] = got[s][: 2 * HD, 768:]
    finish(
        started(
            [
                pltpu.make_async_copy(far, far_hbm, sems.at[0]),
                pltpu.make_async_copy(far.at[:, pl.ds(1024, 512)], farther_hbm, sems.at[1]),
            ]
        )
    )


def loader(keys, values):
    def load(at, block):
        width = block.shape[1]
        keys[:HD, at : at + width] = block[:HD]
        values[:HD, at : at + width] = block[HD:]

    return load


def joined_unit(got, outs, keys, values, parts):
    def query():
        blocks = [got[s][2 * HD :, lanes] for s, lanes in parts]
        return blocks[0] if len(blocks) == 1 else jnp.concatenate(blocks, axis=1)

    def done(sums, top):
        result, at = divided(sums), 0
        for s, lanes in parts:
            width = lanes.stop - lanes.start
            outs[s][:, lanes] = result[:, at : at + width]
            at += width

    return (query, lambda: keys[...], lambda: values[...], done)


def attend1_kernel(*refs):
    got, outs, (keys, values) = refs[:4], refs[4:8], refs[8:]
    load = loader(keys, values)
    for s in range(4):
        load(s * 512, got[s][: 2 * HD, :512])
    finish_keys(keys, values)
    attend(
        [
            joined_unit(got, outs, keys, values, [(s, slice(t * QT, (t + 1) * QT))])
            for s in range(4)
            for t in range(512 // QT)
        ]
    )


def attend23_kernel(*refs):
    got, (x4, x8, x12), first = refs[:4], refs[4:7], refs[7:11]
    outs, (keys, values, sent, sems) = refs[11:15], refs[15:]
    two, three = (keys.at[0], values.at[0]), (keys.at[1], values.at[1])
    for s in range(4):
        loader(*two)(s * 256, got[s][: 2 * HD, 512:768])
        loader(*three)(s * 128, got[s][: 2 * HD, 768:])
    loader(*two)(1024, x4[:, :1024])
    loader(*three)(512, x4[:, 1024:])
    loader(*three)(1024, x8[...])
    loader(*three)(1536, x12[...])
    finish_keys(*two)
    finish_keys(*three)
    made = [outs[0]] + [sent.at[m] for m in range(3)]
    for s in range(4):
        made[s][:, :512] = first[s][...]
    units = [joined_unit(got, made, *two, [(s, slice(512, 768))]) for s in range(4)]
    for s in (0, 2):
        lanes = slice(768, 896)
        units.append(joined_unit(got, made, *three, [(s, lanes), (s + 1, lanes)]))
    attend(units)
    finish(
        started([pltpu.make_async_copy(made[m], outs[m], sems.at[m - 1]) for m in range(1, 4)])
    )


def mlp_kernel(
    off_ref,
    me_ref,
    slots_ref,
    a0_ref,
    aa_ref,
    ab_ref,
    ac_ref,
    ad_ref,
    gain_ref,
    out_weight_hbm,
    up_hbm,
    down_hbm,
    out_hbm,
    attn,
    wide,
    out_weight,
    up,
    down,
    out,
    sems,
    out_sems,
):
    tile, part = 256, 768
    tiles, parts = SLOTS // tile, FF // part
    first = started([pltpu.make_async_copy(out_weight_hbm, out_weight, sems.at[2, 0])])
    loads = []
    for f in range(parts):
        span = slice(f * part, (f + 1) * part)
        loads.append(
            started(
                [
                    pltpu.make_async_copy(up_hbm.at[:, span], up.at[:, span], sems.at[0, f]),
                    pltpu.make_async_copy(down_hbm.at[span, :], down.at[span, :], sems.at[1, f]),
                ]
            )
        )
    attn[: 4 * HD, :] = a0_ref[...]
    attn[4 * HD :, :] = jnp.zeros((12 * HD, SLOTS), BF)

    def lanes(rank):
        return pl.ds(pl.multiple_of(rank * OWNERS, OWNERS), OWNERS)

    for m, ref in enumerate((aa_ref, ab_ref, ac_ref, ad_ref)):
        place = lax.bitwise_xor(me_ref[0] % 4, m)
        for group, start, count in GROUPS:
            head = 4 * group + place
            rows = pl.ds(pl.multiple_of(head * HD, 16), HD)
            for i in range(count):
                attn[rows, lanes(off_ref[head] + 2**group * i)] = ref[
                    :, start + i * 128 : start + (i + 1) * 128
                ]

    finish(first)
    for t in range(tiles):
        mixed = lax.dot_general(
            attn[:, t * tile : (t + 1) * tile], out_weight[...], TN, preferred_element_type=F32
        )
        for i in range(tile // OWNERS):
            r = t * (tile // OWNERS) + i
            for c in range(D // 128):
                wide[c, pl.ds(r, OWNERS, stride=CAP), :] = mixed[
                    i * OWNERS : (i + 1) * OWNERS, c * 128 : (c + 1) * 128
                ]
    gain = row_of(gain_ref)

    def begin(t):
        span = slice(t * tile, (t + 1) * tile)
        rows = slots_ref[span, :].astype(F32)
        held = rows[:, :1] < LIMIT
        mixed = jnp.concatenate([wide[c, span, :] for c in range(D // 128)], axis=1)
        hidden = jnp.where(held, rows, 0.0) + mixed
        centred, scale = normalise(hidden)
        return held, hidden, (centred * scale * gain).astype(BF)

    def raised(normed, f):
        return jnp.dot(normed, up[:, f * part : (f + 1) * part], preferred_element_type=F32)

    state = begin(0)
    loads[0][0].wait()
    act = raised(state[2], 0)
    copies = []
    for t in range(tiles):
        held, hidden, normed = state
        final = hidden
        for f in range(parts):
            if f + 1 < parts:
                if t == 0:
                    loads[f + 1][0].wait()
                following = raised(normed, f + 1)
            elif t + 1 < tiles:
                following = raised(state[2], 0)
            if f == parts - 2 and t + 1 < tiles:
                state = begin(t + 1)
            if t == 0:
                loads[f][1].wait()
            final = final + jnp.dot(
                jax.nn.gelu(act).astype(BF),
                down[f * part : (f + 1) * part, :],
                preferred_element_type=F32,
            )
            act = following
        span = pl.ds(t * tile, tile)
        out[span, :] = jnp.where(held, final, 0.0).astype(BF)
        copies += started(
            [pltpu.make_async_copy(out.at[span], out_hbm.at[0, span], out_sems.at[t])]
        )
    finish(copies)


def grad_kernel(dest_ref, feats_hbm, gain_ref, weight_hbm, back_ref, out_ref, feats, weight, sems):
    loads = [
        pltpu.make_async_copy(weight_hbm, weight, sems.at[0]),
        pltpu.make_async_copy(feats_hbm, feats, sems.at[1]),
    ]
    for load in loads:
        load.start()
    dest = dest_ref[...]
    slot = (dest * CAP + rank_of(dest)).astype(F32)
    slot = jnp.broadcast_to(slot, (128, TILES)).T[:, :1].astype(jnp.int32)
    place = (iota((TILES, SLOTS), 1) == slot).astype(F32).astype(BF)
    rows = jnp.dot(place, back_ref[...], preferred_element_type=F32).astype(BF)
    loads[0].wait()
    grad = lax.dot_general(rows, weight[...], NT, preferred_element_type=F32)
    grad = grad * row_of(gain_ref)
    loads[1].wait()
    centred, scale = normalise(feats[...].astype(F32))
    unit = centred * scale
    along = jnp.mean(grad * unit, axis=-1, keepdims=True)
    level = jnp.mean(grad, axis=-1, keepdims=True)
    out_ref[...] = (scale * (grad - level - unit * along)).astype(BF)


def per_device(
    tile_feats,
    tile_gain,
    proj_weight,
    proj_bias,
    dest,
    slot_gain,
    qkv_weight,
    out_weight,
    mlp_gain,
    up_weight,
    down_weight,
    offsets,
    slot_grad,
):
    sds = jax.ShapeDtypeStruct
    everyone = ("tile", "seq")
    me = lax.axis_index("seq").astype(jnp.int32).reshape(1)
    dest = dest.reshape(1, TILES)
    order = lax.optimization_barrier

    outgoing = call(
        embed_kernel,
        sds((SLOTS, D), BF),
        (pltpu.VMEM((TILES, DT), BF), pltpu.VMEM((DT, D), BF), pltpu.VMEM((SLOTS, D), BF), DMA((3,))),
        60,
        2 * 10**9,
        "embed_tiles",
        [VM, HBM, VM, HBM, VM],
        HBM,
    )(dest, tile_feats, tile_gain, proj_weight, proj_bias)
    outgoing, qkv_weight = order((outgoing, qkv_weight))
    slots = lax.all_to_all(outgoing, everyone, split_axis=0, concat_axis=0, tiled=True)
    turned = call(turn_kernel, sds((3 * D, D), BF), (), 60, 8 * 10**9, "turn_qkv_weight")(
        qkv_weight
    )
    slots, turned, slot_grad = order((slots, turned, slot_grad))
    returned = lax.all_to_all(slot_grad[0], everyone, split_axis=0, concat_axis=0, tiled=True)

    part = sds((3 * HD, TAKEN), BF)
    kv0_shape = sds((8 * HD, SLOTS), BF)
    q0, kv0, *parts, kv0_sent = call(
        qkv_kernel,
        (sds((4 * HD, SLOTS), BF), kv0_shape, part, part, part, part, kv0_shape),
        (
            pltpu.VMEM((D // 128, SLOTS, 128), F32),
            pltpu.VMEM((3 * D, SLOTS), BF),
            pltpu.VMEM((3 * D, D), BF),
            pltpu.VMEM((3, 3 * HD, TAKEN), BF),
            DMA((6,)),
        ),
        VMEM,
        4 * 10**9,
        "make_qkv",
        [SM, SM, VM, VM, HBM],
        (VM, VM, VM, HBM, HBM, HBM, HBM),
    )(offsets, me, slots, slot_gain, turned)

    def send(array, m):
        return lax.ppermute(array, "seq", [(i, i ^ m) for i in range(N_SEQ)])

    one_head = (pltpu.VMEM((64, KEYS), BF), pltpu.VMEM((64, KEYS), BF))
    two_heads = (pltpu.VMEM((2, 64, KEYS), BF), pltpu.VMEM((2, 64, KEYS), BF))
    four_heads = (pltpu.VMEM((4, 64, SLOTS), BF), pltpu.VMEM((4, 64, SLOTS), BF))
    parts = [parts[0]] + [send(parts[m], m) for m in range(1, 4)]
    other = send(kv0_sent, 1)
    half = call(
        own_half_kernel, sds((4, 64, SLOTS), F32), four_heads, VMEM, 8 * 10**9, "attend_own_half"
    )(q0, kv0)
    returned, half = order((returned, half))
    tile_grad = call(
        grad_kernel,
        sds((TILES, DT), BF),
        (pltpu.VMEM((TILES, DT), BF), pltpu.VMEM((DT, D), BF), DMA((2,))),
        56,
        4 * 10**9,
        "tile_cotangent",
        [VM, HBM, VM, HBM, VM],
    )(dest, tile_feats, tile_gain, proj_weight, returned)
    tile_grad, half, *parts = order((tile_grad, half, *parts))
    far, farther = call(
        pack_kernel,
        (sds((2 * HD, 1536), BF), sds((2 * HD, 512), BF)),
        (pltpu.VMEM((2 * HD, 1536), BF), DMA((2,))),
        VMEM,
        10**9,
        "pack_far_keys",
        None,
        (HBM, HBM),
    )(*parts)
    x4, x8, x12 = send(far, 4), send(farther, 8), send(farther, 12)
    result = sds((HD, TAKEN), BF)
    first = call(
        attend1_kernel, (sds((HD, 512), BF),) * 4, one_head, VMEM, 8 * 10**9, "attend_group1"
    )(*parts)
    x4, x8, x12, *first = order((x4, x8, x12, *first))
    rest = call(
        attend23_kernel,
        (result,) * 4,
        two_heads + (pltpu.VMEM((3, HD, TAKEN), BF), DMA((3,))),
        VMEM,
        6 * 10**9,
        "attend_groups23",
        None,
        (VM, HBM, HBM, HBM),
    )(*parts, x4, x8, x12, *first)
    other, half, *rest = order((other, half, *rest))
    rest = [rest[0]] + [send(rest[m], m) for m in range(1, 4)]
    a0 = call(
        other_half_kernel, sds((4 * HD, SLOTS), BF), four_heads, VMEM, 8 * 10**9, "attend_other_half"
    )(q0, other, half)
    a0, *rest = order((a0, *rest))

    slide_states = call(
        mlp_kernel,
        sds((1, SLOTS, D), BF),
        (
            pltpu.VMEM((D, SLOTS), BF),
            pltpu.VMEM((D // 128, SLOTS, 128), F32),
            pltpu.VMEM((D, D), BF),
            pltpu.VMEM((D, FF), BF),
            pltpu.VMEM((FF, D), BF),
            pltpu.VMEM((SLOTS, D), BF),
            DMA((3, 4)),
            DMA((4,)),
        ),
        58,
        11 * 10**9,
        "out_and_mlp",
        [SM, SM] + [VM] * 7 + [HBM] * 3,
        HBM,
    )(offsets, me, slots, a0, *rest, mlp_gain, out_weight, up_weight, down_weight)
    return (slide_states, tile_grad)


def solution(mesh):
    return jax.shard_map(
        per_device,
        mesh=mesh,
        in_specs=(
            P(("tile", "seq"), None),
            P(),
            P(),
            P(),
            P(("tile", "seq"), None),
            P(),
            P(),
            P(),
            P(),
            P(),
            P(),
            P(),
            P("tile", "seq", None),
        ),
        out_specs=(P("tile", "seq", None), P(("tile", "seq"), None)),
        check_vma=False,
    )
```

```python
import math

import jax
import jax.numpy as jnp
from jax import lax
from jax.experimental import pallas as pl
from jax.experimental.pallas import tpu as pltpu
from jax.sharding import PartitionSpec as P

DT = 1536
D = 768
HEADS = 16
FF = 3072
HD = 48
TILES = 512
CAP = 8
OWNERS = 128
SLOTS = 1024
KEYS = 2048
N_SEQ = 16
EPS = 1e-05
MIB = 2**20
VMEM = 32

EMPTY = 3e38
LIMIT = 1e37
MASKED = -1e30
SCALE = HD**-0.5 * math.log2(math.e)

BF = jnp.bfloat16
F32 = jnp.float32
NT = (((1,), (1,)), ((), ()))
TN = (((0,), (0,)), ((), ()))


def iota(shape, axis):
    return lax.broadcasted_iota(jnp.int32, shape, axis)


def normalise(values):
    mean = jnp.mean(values, axis=-1, keepdims=True)
    centred = values - mean
    spread = jnp.mean(centred * centred, axis=-1, keepdims=True)
    return centred, lax.rsqrt(spread + EPS)


def call(kernel, outs, scratch, vmem, flops, name, in_specs=None, out_specs=None):
    specs = {} if in_specs is None else {"in_specs": in_specs}
    if out_specs is not None:
        specs["out_specs"] = out_specs
    return pl.pallas_call(
        kernel,
        out_shape=outs,
        **specs,
        scratch_shapes=scratch,
        name=name,
        compiler_params=pltpu.CompilerParams(vmem_limit_bytes=vmem * MIB),
        cost_estimate=pl.CostEstimate(flops=flops, bytes_accessed=8 * MIB, transcendentals=0),
    )


VM = pl.BlockSpec(memory_space=pltpu.VMEM)
SM = pl.BlockSpec(memory_space=pltpu.SMEM)
HBM = pl.BlockSpec(memory_space=pltpu.HBM)
DMA = pltpu.SemaphoreType.DMA


def started(copies):
    for copy in copies:
        copy.start()
    return copies


def finish(copies):
    for copy in copies:
        copy.wait()


GROUPS = ((1, 0, 4), (2, 512, 2), (3, 768, 1))
TAKEN = 896


def row_of(ref):
    return ref[...].reshape(1, ref.shape[0])


def rank_of(dest):
    hot = (iota((OWNERS, TILES), 0) == dest).astype(F32)
    earlier = (iota((TILES, TILES), 0) < iota((TILES, TILES), 1)).astype(F32).astype(BF)
    before = jnp.dot(hot.astype(BF), earlier, preferred_element_type=F32)
    return jnp.sum(before * hot, axis=0, keepdims=True).astype(jnp.int32)


def embed_kernel(
    dest_ref, feats_hbm, gain_ref, weight_hbm, bias_ref, out_hbm, feats, weight, out, sems
):
    loads = started(
        [
            pltpu.make_async_copy(feats_hbm, feats, sems.at[0]),
            pltpu.make_async_copy(weight_hbm, weight, sems.at[1]),
        ]
    )
    dest = dest_ref[...]
    place = (iota((SLOTS, TILES), 0) == dest * CAP + rank_of(dest)).astype(F32)
    taken = jnp.max(place, axis=1, keepdims=True)
    place = place.astype(BF)
    loads[0].wait()
    centred, scale = normalise(feats[...].astype(F32))
    normed = (centred * scale * row_of(gain_ref)).astype(BF)
    loads[1].wait()
    emb = jnp.dot(normed, weight[...], preferred_element_type=F32) + row_of(bias_ref)
    rows = jnp.dot(place, emb.astype(BF), preferred_element_type=F32)
    out[...] = jnp.where(taken > 0, rows, EMPTY).astype(BF)
    finish(started([pltpu.make_async_copy(out, out_hbm, sems.at[2])]))


def turn_kernel(weight_ref, out_ref):
    for i in range(6):
        cols = slice(i * 384, (i + 1) * 384)
        out_ref[cols, :] = weight_ref[:, cols].T


def qkv_kernel(
    off_ref,
    me_ref,
    slots_ref,
    gain_ref,
    weight_hbm,
    q0_ref,
    kv0_ref,
    sa_ref,
    sb_hbm,
    sc_hbm,
    sd_hbm,
    kv0_hbm,
    wide,
    mixed,
    weight,
    sent,
    sems,
):
    loads = started([pltpu.make_async_copy(weight_hbm, weight, sems.at[0])])
    for c in range(D // 128):
        wide[c] = slots_ref[:, c * 128 : (c + 1) * 128].astype(F32)
    gain = row_of(gain_ref)

    def prepared(block):
        flags, normed = [], []
        for r in (2 * block, 2 * block + 1):
            rows = jnp.concatenate(
                [wide[c, pl.ds(r, OWNERS, stride=CAP), :] for c in range(D // 128)], axis=1
            )
            held = rows[:, :1] < LIMIT
            flags.append(jnp.broadcast_to(held.astype(F32), (OWNERS, 128)).T[:1])
            centred, scale = normalise(jnp.where(held, rows, 0.0))
            normed.append((centred * scale * gain).astype(BF))
        return jnp.concatenate(flags, axis=1) > 0, jnp.concatenate(normed, axis=0)

    state = prepared(0)
    finish(loads)
    for block in range(4):
        held, normed = state
        if block < 3:
            state = prepared(block + 1)
        lanes = slice(block * 256, (block + 1) * 256)
        for part in range(3):
            rows = slice(part * D, (part + 1) * D)
            made = lax.dot_general(weight[rows, :], normed, NT, preferred_element_type=F32)
            if part == 0:
                made = made * SCALE
            if part == 1:
                made = jnp.where(held, made, EMPTY)
            mixed[rows, lanes] = made.astype(BF)
    copies = started(
        [
            pltpu.make_async_copy(mixed.at[pl.ds(D, 4 * HD)], kv0_hbm.at[pl.ds(0, 4 * HD)], sems.at[1]),
            pltpu.make_async_copy(
                mixed.at[pl.ds(2 * D, 4 * HD)], kv0_hbm.at[pl.ds(4 * HD, 4 * HD)], sems.at[2]
            ),
        ]
    )

    def piece(part, head, rank):
        lanes = pl.ds(pl.multiple_of(rank * OWNERS, OWNERS), OWNERS)
        return mixed[pl.ds(pl.multiple_of(part * D + head * HD, 16), HD), lanes]

    for m in (1, 2, 3, 0):
        ref = sent.at[m - 1] if m else sa_ref
        place = lax.bitwise_xor(me_ref[0] % 4, m)
        for group, start, count in GROUPS:
            head = 4 * group + place
            for row, part in enumerate((1, 2, 0)):
                for i in range(count):
                    ref[row * HD : (row + 1) * HD, start + i * 128 : start + (i + 1) * 128] = piece(
                        part, head, off_ref[head] + 2**group * i
                    )
        if m:
            target = (sb_hbm, sc_hbm, sd_hbm)[m - 1]
            copies += started([pltpu.make_async_copy(ref, target, sems.at[2 + m])])
    q0_ref[...] = mixed[0 : 4 * HD, :]
    kv0_ref[0 : 4 * HD, :] = mixed[D : D + 4 * HD, :]
    kv0_ref[4 * HD :, :] = mixed[2 * D : 2 * D + 4 * HD, :]
    finish(copies)


def finish_keys(keys, values):
    width = keys.shape[1]
    top = iota((16, width), 0) == 0
    empty = keys[0:1, :].astype(F32) > LIMIT
    keys[HD:, :] = jnp.where(top & empty, MASKED, 0.0).astype(BF)
    keys[:HD, :] = jnp.where(empty, 0.0, keys[:HD, :].astype(F32)).astype(BF)
    values[HD:, :] = jnp.where(top, 1.0, 0.0).astype(BF)


def with_ones(query):
    width = query.shape[1]
    ones = jnp.where(iota((16, width), 0) == 0, 1.0, 0.0).astype(BF)
    return jnp.concatenate([query, ones], axis=0)


def attend(units):
    def score(unit):
        return jnp.dot(with_ones(unit[0]()).T, unit[1](), preferred_element_type=F32)

    scores = score(units[0])
    for i, unit in enumerate(units):
        top = jnp.max(scores, axis=1, keepdims=True)
        later = score(units[i + 1]) if i + 1 < len(units) else None
        weights = jnp.exp2(scores - top).astype(BF)
        sums = lax.dot_general(weights, unit[2](), NT, preferred_element_type=F32)
        unit[3](sums, top)
        scores = later


def divided(sums):
    turned = sums.T
    return (turned[:HD] / jnp.maximum(turned[HD : HD + 1], 1e-30)).astype(BF)


QT = 256


def units0(q_ref, keys, values, done):
    units = []
    for head in range(4):
        for t in range(SLOTS // QT):
            rows, lanes = slice(head * HD, (head + 1) * HD), slice(t * QT, (t + 1) * QT)
            units.append(
                (
                    lambda rows=rows, lanes=lanes: q_ref[rows, lanes],
                    lambda head=head: keys[head],
                    lambda head=head: values[head],
                    lambda sums, top, at=(head, rows, lanes): done(sums, top, *at),
                )
            )
    return units


def load0(kv_ref, keys, values):
    for head in range(4):
        keys[head, :HD] = kv_ref[head * HD : (head + 1) * HD, :]
        values[head, :HD] = kv_ref[(4 + head) * HD : (5 + head) * HD, :]
        finish_keys(keys.at[head], values.at[head])


def own_half_kernel(q_ref, kv_ref, out_ref, keys, values):
    load0(kv_ref, keys, values)

    def done(sums, top, head, rows, lanes):
        turned = jnp.where(iota((QT, 64), 1) == HD + 1, top, sums).T
        out_ref[head, :, lanes] = turned

    attend(units0(q_ref, keys, values, done))


def other_half_kernel(q_ref, kv_ref, half_ref, out_ref, keys, values):
    load0(kv_ref, keys, values)

    def done(sums, top, head, rows, lanes):
        mine = jnp.where(iota((QT, 64), 1) == HD + 1, top, sums).T
        before = half_ref[head, :, lanes]
        top_mine, top_before = mine[HD + 1 : HD + 2], before[HD + 1 : HD + 2]
        top = jnp.maximum(top_mine, top_before)
        total = mine * jnp.exp2(top_mine - top) + before * jnp.exp2(top_before - top)
        out_ref[rows, lanes] = (total[:HD] / jnp.maximum(total[HD : HD + 1], 1e-30)).astype(BF)

    attend(units0(q_ref, keys, values, done))


def pack_kernel(*refs):
    got, (far_hbm, farther_hbm, far, sems) = refs[:4], refs[4:]
    for s in range(4):
        far[:, s * 256 : (s + 1) * 256] = got[s][: 2 * HD, 512:768]
        far[:, 1024 + s * 128 : 1024 + (s + 1) * 128] = got[s][: 2 * HD, 768:]
    finish(
        started(
            [
                pltpu.make_async_copy(far, far_hbm, sems.at[0]),
                pltpu.make_async_copy(far.at[:, pl.ds(1024, 512)], farther_hbm, sems.at[1]),
            ]
        )
    )


def loader(keys, values):
    def load(at, block):
        width = block.shape[1]
        keys[:HD, at : at + width] = block[:HD]
        values[:HD, at : at + width] = block[HD:]

    return load


def joined_unit(got, outs, keys, values, parts):
    def query():
        blocks = [got[s][2 * HD :, lanes] for s, lanes in parts]
        return blocks[0] if len(blocks) == 1 else jnp.concatenate(blocks, axis=1)

    def done(sums, top):
        result, at = divided(sums), 0
        for s, lanes in parts:
            width = lanes.stop - lanes.start
            outs[s][:, lanes] = result[:, at : at + width]
            at += width

    return (query, lambda: keys[...], lambda: values[...], done)


def attend1_kernel(*refs):
    got, outs, (keys, values) = refs[:4], refs[4:8], refs[8:]
    load = loader(keys, values)
    for s in range(4):
        load(s * 512, got[s][: 2 * HD, :512])
    finish_keys(keys, values)
    attend(
        [
            joined_unit(got, outs, keys, values, [(s, slice(t * QT, (t + 1) * QT))])
            for s in range(4)
            for t in range(512 // QT)
        ]
    )


def attend23_kernel(*refs):
    got, (x4, x8, x12), first = refs[:4], refs[4:7], refs[7:11]
    outs, (keys, values, sent, sems) = refs[11:15], refs[15:]
    two, three = (keys.at[0], values.at[0]), (keys.at[1], values.at[1])
    for s in range(4):
        loader(*two)(s * 256, got[s][: 2 * HD, 512:768])
        loader(*three)(s * 128, got[s][: 2 * HD, 768:])
    loader(*two)(1024, x4[:, :1024])
    loader(*three)(512, x4[:, 1024:])
    loader(*three)(1024, x8[...])
    loader(*three)(1536, x12[...])
    finish_keys(*two)
    finish_keys(*three)
    made = [outs[0]] + [sent.at[m] for m in range(3)]
    for s in range(4):
        made[s][:, :512] = first[s][...]
    units = [joined_unit(got, made, *two, [(s, slice(512, 768))]) for s in range(4)]
    for s in (0, 2):
        lanes = slice(768, 896)
        units.append(joined_unit(got, made, *three, [(s, lanes), (s + 1, lanes)]))
    attend(units)
    finish(
        started([pltpu.make_async_copy(made[m], outs[m], sems.at[m - 1]) for m in range(1, 4)])
    )


def mlp_kernel(
    off_ref,
    me_ref,
    slots_hbm,
    a0_ref,
    aa_ref,
    ab_ref,
    ac_ref,
    ad_ref,
    gain_ref,
    out_weight_hbm,
    up_hbm,
    down_hbm,
    out_hbm,
    attn,
    wide,
    slots,
    out_weight,
    up,
    down,
    out,
    sems,
    out_sems,
):
    part = 768
    parts = FF // part
    first = started([pltpu.make_async_copy(out_weight_hbm, out_weight, sems.at[2, 0])])
    residual = started([pltpu.make_async_copy(slots_hbm, slots, sems.at[2, 1])])
    loads = []
    for f in range(parts):
        span = slice(f * part, (f + 1) * part)
        loads.append(
            started(
                [
                    pltpu.make_async_copy(up_hbm.at[:, span], up.at[:, span], sems.at[0, f]),
                    pltpu.make_async_copy(down_hbm.at[span, :], down.at[span, :], sems.at[1, f]),
                ]
            )
        )
    attn[: 4 * HD, :] = a0_ref[...]
    attn[4 * HD :, :] = jnp.zeros((12 * HD, SLOTS), BF)

    def lanes(rank):
        return pl.ds(pl.multiple_of(rank * OWNERS, OWNERS), OWNERS)

    for m, ref in enumerate((aa_ref, ab_ref, ac_ref, ad_ref)):
        place = lax.bitwise_xor(me_ref[0] % 4, m)
        for group, start, count in GROUPS:
            head = 4 * group + place
            rows = pl.ds(pl.multiple_of(head * HD, 16), HD)
            for i in range(count):
                attn[rows, lanes(off_ref[head] + 2**group * i)] = ref[
                    :, start + i * 128 : start + (i + 1) * 128
                ]

    finish(first)
    for t in range(4):
        mixed = lax.dot_general(
            attn[:, t * 256 : (t + 1) * 256], out_weight[...], TN, preferred_element_type=F32
        )
        for i in range(2):
            for c in range(D // 128):
                wide[c, pl.ds(2 * t + i, OWNERS, stride=CAP), :] = mixed[
                    i * OWNERS : (i + 1) * OWNERS, c * 128 : (c + 1) * 128
                ]
    gain = row_of(gain_ref)
    finish(residual)
    for load in loads:
        finish(load)
    tile = 512

    def written(t):
        span = pl.ds(pl.multiple_of(t * tile, tile), tile)
        return pltpu.make_async_copy(out.at[span], out_hbm.at[0, span], out_sems.at[t])

    def step(t, carry):
        span = pl.ds(pl.multiple_of(t * tile, tile), tile)
        rows = slots[span, :].astype(F32)
        held = rows[:, :1] < LIMIT
        mixed = jnp.concatenate([wide[c, span, :] for c in range(D // 128)], axis=1)
        hidden = jnp.where(held, rows, 0.0) + mixed
        centred, scale = normalise(hidden)
        normed = (centred * scale * gain).astype(BF)

        def raised(f):
            return jnp.dot(normed, up[:, f * part : (f + 1) * part], preferred_element_type=F32)

        final, act = hidden, raised(0)
        for f in range(parts):
            following = raised(f + 1) if f + 1 < parts else None
            final = final + jnp.dot(
                jax.nn.gelu(act).astype(BF),
                down[f * part : (f + 1) * part, :],
                preferred_element_type=F32,
            )
            act = following
        out[span, :] = jnp.where(held, final, 0.0).astype(BF)
        written(t).start()
        return carry

    lax.fori_loop(0, SLOTS // tile, step, 0)
    finish([written(t) for t in range(SLOTS // tile)])


def grad_kernel(
    dest_ref, feats_hbm, gain_ref, weight_hbm, back_hbm, out_hbm, feats, weight, back, out, sems
):
    loads = started(
        [
            pltpu.make_async_copy(back_hbm, back, sems.at[6]),
            pltpu.make_async_copy(weight_hbm, weight, sems.at[0]),
            pltpu.make_async_copy(feats_hbm, feats, sems.at[1]),
        ]
    )
    dest = dest_ref[...]
    slot = (dest * CAP + rank_of(dest)).astype(F32)
    slot = jnp.broadcast_to(slot, (128, TILES)).T[:, :1].astype(jnp.int32)
    gain = row_of(gain_ref)
    copies = []
    for t in range(2):
        span = slice(t * 256, (t + 1) * 256)
        place = (iota((256, SLOTS), 1) == slot[span]).astype(F32).astype(BF)
        if t == 0:
            loads[0].wait()
        rows = jnp.dot(place, back[...], preferred_element_type=F32).astype(BF)
        if t == 0:
            loads[1].wait()
        grad = lax.dot_general(rows, weight[...], NT, preferred_element_type=F32) * gain
        if t == 0:
            loads[2].wait()
        centred, scale = normalise(feats[span, :].astype(F32))
        unit = centred * scale
        along = jnp.mean(grad * unit, axis=-1, keepdims=True)
        level = jnp.mean(grad, axis=-1, keepdims=True)
        out[span, :] = (scale * (grad - level - unit * along)).astype(BF)
        part = pl.ds(t * 256, 256)
        copies += started([pltpu.make_async_copy(out.at[part], out_hbm.at[part], sems.at[2 + t])])
    finish(copies)


def per_device(
    tile_feats,
    tile_gain,
    proj_weight,
    proj_bias,
    dest,
    slot_gain,
    qkv_weight,
    out_weight,
    mlp_gain,
    up_weight,
    down_weight,
    offsets,
    slot_grad,
):
    sds = jax.ShapeDtypeStruct

    def in_hbm(array):
        return pltpu.with_memory_space_constraint(array, pltpu.HBM)

    def in_vmem(array):
        return pltpu.with_memory_space_constraint(array, pltpu.VMEM)

    everyone = ("tile", "seq")
    me = lax.axis_index("seq").astype(jnp.int32).reshape(1)
    dest = dest.reshape(1, TILES)
    order = lax.optimization_barrier

    outgoing = call(
        embed_kernel,
        sds((SLOTS, D), BF),
        (pltpu.VMEM((TILES, DT), BF), pltpu.VMEM((DT, D), BF), pltpu.VMEM((SLOTS, D), BF), DMA((3,))),
        VMEM,
        2 * 10**9,
        "embed_tiles",
        [VM, HBM, VM, HBM, VM],
        HBM,
    )(
        in_hbm(dest),
        in_hbm(tile_feats),
        in_hbm(tile_gain),
        in_hbm(proj_weight),
        in_hbm(proj_bias),
    )
    outgoing, qkv_weight = order((outgoing, qkv_weight))
    slots = lax.all_to_all(outgoing, everyone, split_axis=0, concat_axis=0, tiled=True)
    turned = call(turn_kernel, sds((3 * D, D), BF), (), VMEM, 8 * 10**9, "turn_qkv_weight")(
        qkv_weight
    )
    slots, turned, slot_grad = order((slots, turned, slot_grad))
    turned = in_hbm(turned)
    returned = lax.all_to_all(slot_grad[0], everyone, split_axis=0, concat_axis=0, tiled=True)

    part = sds((3 * HD, TAKEN), BF)
    kv0_shape = sds((8 * HD, SLOTS), BF)
    q0, kv0, *parts, kv0_sent = call(
        qkv_kernel,
        (sds((4 * HD, SLOTS), BF), kv0_shape, part, part, part, part, kv0_shape),
        (
            pltpu.VMEM((D // 128, SLOTS, 128), F32),
            pltpu.VMEM((3 * D, SLOTS), BF),
            pltpu.VMEM((3 * D, D), BF),
            pltpu.VMEM((3, 3 * HD, TAKEN), BF),
            DMA((6,)),
        ),
        VMEM,
        4 * 10**9,
        "make_qkv",
        [SM, SM, VM, VM, HBM],
        (VM, VM, VM, HBM, HBM, HBM, HBM),
    )(offsets, me, slots, in_hbm(slot_gain), turned)

    def send(array, m):
        return lax.ppermute(array, "seq", [(i, i ^ m) for i in range(N_SEQ)])

    one_head = (pltpu.VMEM((64, KEYS), BF), pltpu.VMEM((64, KEYS), BF))
    two_heads = (pltpu.VMEM((2, 64, KEYS), BF), pltpu.VMEM((2, 64, KEYS), BF))
    four_heads = (pltpu.VMEM((4, 64, SLOTS), BF), pltpu.VMEM((4, 64, SLOTS), BF))
    parts = [parts[0]] + [send(parts[m], m) for m in range(1, 4)]
    other = send(kv0_sent, 1)
    half = call(
        own_half_kernel, sds((4, 64, SLOTS), F32), four_heads, VMEM, 8 * 10**9, "attend_own_half"
    )(q0, kv0)
    returned, half = order((returned, half))
    tile_grad = call(
        grad_kernel,
        sds((TILES, DT), BF),
        (
            pltpu.VMEM((TILES, DT), BF),
            pltpu.VMEM((DT, D), BF),
            pltpu.VMEM((SLOTS, D), BF),
            pltpu.VMEM((TILES, DT), BF),
            DMA((7,)),
        ),
        56,
        4 * 10**9,
        "tile_cotangent",
        [VM, HBM, VM, HBM, HBM],
        HBM,
    )(
        in_hbm(dest),
        in_hbm(tile_feats),
        in_hbm(tile_gain),
        in_hbm(proj_weight),
        in_hbm(returned),
    )
    tile_grad, half, *parts = order((tile_grad, half, *parts))
    parts = [in_vmem(array) for array in parts]
    far, farther = call(
        pack_kernel,
        (sds((2 * HD, 1536), BF), sds((2 * HD, 512), BF)),
        (pltpu.VMEM((2 * HD, 1536), BF), DMA((2,))),
        VMEM,
        10**9,
        "pack_far_keys",
        None,
        (HBM, HBM),
    )(*parts)
    x12, x8, x4 = send(farther, 12), send(farther, 8), send(far, 4)
    result = sds((HD, TAKEN), BF)
    first = call(
        attend1_kernel, (sds((HD, 512), BF),) * 4, one_head, VMEM, 8 * 10**9, "attend_group1"
    )(*parts)
    x4, x8, x12, *first = order((x4, x8, x12, *first))
    rest = call(
        attend23_kernel,
        (result,) * 4,
        two_heads + (pltpu.VMEM((3, HD, TAKEN), BF), DMA((3,))),
        VMEM,
        6 * 10**9,
        "attend_groups23",
        None,
        (VM, HBM, HBM, HBM),
    )(*parts, x4, x8, x12, *first)
    other, half, *rest = order((other, half, *rest))
    rest = [rest[0]] + [send(rest[m], m) for m in range(1, 4)]
    a0 = call(
        other_half_kernel, sds((4 * HD, SLOTS), BF), four_heads, VMEM, 8 * 10**9, "attend_other_half"
    )(in_vmem(q0), in_vmem(other), in_vmem(half))
    a0, *rest = order((a0, *rest))

    slide_states = call(
        mlp_kernel,
        sds((1, SLOTS, D), BF),
        (
            pltpu.VMEM((D, SLOTS), BF),
            pltpu.VMEM((D // 128, SLOTS, 128), F32),
            pltpu.VMEM((SLOTS, D), BF),
            pltpu.VMEM((D, D), BF),
            pltpu.VMEM((D, FF), BF),
            pltpu.VMEM((FF, D), BF),
            pltpu.VMEM((SLOTS, D), BF),
            DMA((3, 4)),
            DMA((2,)),
        ),
        40,
        11 * 10**9,
        "out_and_mlp",
        [SM, SM, HBM] + [VM] * 6 + [HBM] * 3,
        HBM,
    )(offsets, me, in_hbm(slots), a0, *rest, in_hbm(mlp_gain), in_hbm(out_weight), in_hbm(up_weight), in_hbm(down_weight))
    return (slide_states, tile_grad)


def solution(mesh):
    return jax.shard_map(
        per_device,
        mesh=mesh,
        in_specs=(
            P(("tile", "seq"), None),
            P(),
            P(),
            P(),
            P(("tile", "seq"), None),
            P(),
            P(),
            P(),
            P(),
            P(),
            P(),
            P(),
            P("tile", "seq", None),
        ),
        out_specs=(P("tile", "seq", None), P(("tile", "seq"), None)),
        check_vma=False,
    )
```

```python
import math

import jax
import jax.numpy as jnp
from jax import lax
from jax.experimental import pallas as pl
from jax.experimental.pallas import tpu as pltpu
from jax.sharding import PartitionSpec as P

DT = 1536
D = 768
HEADS = 16
FF = 3072
HD = 48
TILES = 512
CAP = 8
OWNERS = 128
SLOTS = 1024
KEYS = 2048
N_SEQ = 16
EPS = 1e-05
MIB = 2**20
VMEM = 32

EMPTY = 3e38
LIMIT = 1e37
MASKED = -1e30
SCALE = HD**-0.5 * math.log2(math.e)

BF = jnp.bfloat16
F32 = jnp.float32
NT = (((1,), (1,)), ((), ()))
TN = (((0,), (0,)), ((), ()))


def iota(shape, axis):
    return lax.broadcasted_iota(jnp.int32, shape, axis)


def normalise(values):
    mean = jnp.mean(values, axis=-1, keepdims=True)
    centred = values - mean
    spread = jnp.mean(centred * centred, axis=-1, keepdims=True)
    return centred, lax.rsqrt(spread + EPS)


def call(kernel, outs, scratch, vmem, flops, name, in_specs=None, out_specs=None):
    specs = {} if in_specs is None else {"in_specs": in_specs}
    if out_specs is not None:
        specs["out_specs"] = out_specs
    return pl.pallas_call(
        kernel,
        out_shape=outs,
        **specs,
        scratch_shapes=scratch,
        name=name,
        compiler_params=pltpu.CompilerParams(vmem_limit_bytes=vmem * MIB),
        cost_estimate=pl.CostEstimate(flops=flops, bytes_accessed=8 * MIB, transcendentals=0),
    )


VM = pl.BlockSpec(memory_space=pltpu.VMEM)
SM = pl.BlockSpec(memory_space=pltpu.SMEM)
HBM = pl.BlockSpec(memory_space=pltpu.HBM)
DMA = pltpu.SemaphoreType.DMA


def started(copies):
    for copy in copies:
        copy.start()
    return copies


def finish(copies):
    for copy in copies:
        copy.wait()


GROUPS = ((1, 0, 4), (2, 512, 2), (3, 768, 1))
TAKEN = 896


def row_of(ref):
    return ref[...].reshape(1, ref.shape[0])


def rank_of(dest):
    hot = (iota((OWNERS, TILES), 0) == dest).astype(F32)
    earlier = (iota((TILES, TILES), 0) < iota((TILES, TILES), 1)).astype(F32).astype(BF)
    before = jnp.dot(hot.astype(BF), earlier, preferred_element_type=F32)
    return jnp.sum(before * hot, axis=0, keepdims=True).astype(jnp.int32)


def embed_kernel(
    dest_ref, feats_hbm, gain_ref, weight_hbm, bias_ref, out_hbm, feats, weight, out, sems
):
    loads = started(
        [
            pltpu.make_async_copy(feats_hbm, feats, sems.at[0]),
            pltpu.make_async_copy(weight_hbm, weight, sems.at[1]),
        ]
    )
    dest = dest_ref[...]
    place = (iota((SLOTS, TILES), 0) == dest * CAP + rank_of(dest)).astype(F32)
    taken = jnp.max(place, axis=1, keepdims=True)
    place = place.astype(BF)
    gain, bias = row_of(gain_ref), row_of(bias_ref)
    loads[0].wait()
    normed = []
    for t in range(2):
        centred, scale = normalise(feats[t * 256 : (t + 1) * 256, :].astype(F32))
        normed.append((centred * scale * gain).astype(BF))
    loads[1].wait()
    emb = [
        (jnp.dot(part, weight[...], preferred_element_type=F32) + bias).astype(BF)
        for part in normed
    ]
    emb = jnp.concatenate(emb, axis=0)
    copies = []
    for t in range(2):
        span = slice(t * 512, (t + 1) * 512)
        rows = jnp.dot(place[span], emb, preferred_element_type=F32)
        out[span, :] = jnp.where(taken[span] > 0, rows, EMPTY).astype(BF)
        part = pl.ds(t * 512, 512)
        copies += started([pltpu.make_async_copy(out.at[part], out_hbm.at[part], sems.at[2 + t])])
    finish(copies)


def turn_kernel(weight_ref, out_ref):
    for i in range(6):
        cols = slice(i * 384, (i + 1) * 384)
        out_ref[cols, :] = weight_ref[:, cols].T


def qkv_kernel(
    off_ref,
    me_ref,
    slots_ref,
    gain_ref,
    weight_hbm,
    q0_ref,
    kv0_ref,
    sa_ref,
    sb_hbm,
    sc_hbm,
    sd_hbm,
    kv0_hbm,
    wide,
    mixed,
    weight,
    sent,
    sems,
):
    loads = started([pltpu.make_async_copy(weight_hbm, weight, sems.at[0])])
    for c in range(D // 128):
        wide[c] = slots_ref[:, c * 128 : (c + 1) * 128].astype(F32)
    gain = row_of(gain_ref)

    def prepared(block):
        flags, normed = [], []
        for r in (2 * block, 2 * block + 1):
            rows = jnp.concatenate(
                [wide[c, pl.ds(r, OWNERS, stride=CAP), :] for c in range(D // 128)], axis=1
            )
            held = rows[:, :1] < LIMIT
            flags.append(jnp.broadcast_to(held.astype(F32), (OWNERS, 128)).T[:1])
            centred, scale = normalise(jnp.where(held, rows, 0.0))
            normed.append((centred * scale * gain).astype(BF))
        return jnp.concatenate(flags, axis=1) > 0, jnp.concatenate(normed, axis=0)

    state = prepared(0)
    finish(loads)
    for block in range(4):
        held, normed = state
        if block < 3:
            state = prepared(block + 1)
        lanes = slice(block * 256, (block + 1) * 256)
        for part in range(3):
            rows = slice(part * D, (part + 1) * D)
            made = lax.dot_general(weight[rows, :], normed, NT, preferred_element_type=F32)
            if part == 0:
                made = made * SCALE
            if part == 1:
                made = jnp.where(held, made, EMPTY)
            mixed[rows, lanes] = made.astype(BF)
    copies = started(
        [
            pltpu.make_async_copy(mixed.at[pl.ds(D, 4 * HD)], kv0_hbm.at[pl.ds(0, 4 * HD)], sems.at[1]),
            pltpu.make_async_copy(
                mixed.at[pl.ds(2 * D, 4 * HD)], kv0_hbm.at[pl.ds(4 * HD, 4 * HD)], sems.at[2]
            ),
        ]
    )

    def piece(part, head, rank):
        lanes = pl.ds(pl.multiple_of(rank * OWNERS, OWNERS), OWNERS)
        return mixed[pl.ds(pl.multiple_of(part * D + head * HD, 16), HD), lanes]

    for m in (1, 2, 3, 0):
        ref = sent.at[m - 1] if m else sa_ref
        place = lax.bitwise_xor(me_ref[0] % 4, m)
        for group, start, count in GROUPS:
            head = 4 * group + place
            for row, part in enumerate((1, 2, 0)):
                for i in range(count):
                    ref[row * HD : (row + 1) * HD, start + i * 128 : start + (i + 1) * 128] = piece(
                        part, head, off_ref[head] + 2**group * i
                    )
        if m:
            target = (sb_hbm, sc_hbm, sd_hbm)[m - 1]
            copies += started([pltpu.make_async_copy(ref, target, sems.at[2 + m])])
    q0_ref[...] = mixed[0 : 4 * HD, :]
    kv0_ref[0 : 4 * HD, :] = mixed[D : D + 4 * HD, :]
    kv0_ref[4 * HD :, :] = mixed[2 * D : 2 * D + 4 * HD, :]
    finish(copies)


def finish_keys(keys, values):
    width = keys.shape[1]
    top = iota((16, width), 0) == 0
    empty = keys[0:1, :].astype(F32) > LIMIT
    keys[HD:, :] = jnp.where(top & empty, MASKED, 0.0).astype(BF)
    keys[:HD, :] = jnp.where(empty, 0.0, keys[:HD, :].astype(F32)).astype(BF)
    values[HD:, :] = jnp.where(top, 1.0, 0.0).astype(BF)


def with_ones(query):
    width = query.shape[1]
    ones = jnp.where(iota((16, width), 0) == 0, 1.0, 0.0).astype(BF)
    return jnp.concatenate([query, ones], axis=0)


def attend(units):
    def score(unit):
        return jnp.dot(with_ones(unit[0]()).T, unit[1](), preferred_element_type=F32)

    scores = score(units[0])
    for i, unit in enumerate(units):
        top = jnp.max(scores, axis=1, keepdims=True)
        later = score(units[i + 1]) if i + 1 < len(units) else None
        weights = jnp.exp2(scores - top).astype(BF)
        sums = lax.dot_general(weights, unit[2](), NT, preferred_element_type=F32)
        unit[3](sums, top)
        scores = later


def divided(sums):
    turned = sums.T
    return (turned[:HD] / jnp.maximum(turned[HD : HD + 1], 1e-30)).astype(BF)


QT = 256


def units0(q_ref, keys, values, done):
    units = []
    for head in range(4):
        for t in range(SLOTS // QT):
            rows, lanes = slice(head * HD, (head + 1) * HD), slice(t * QT, (t + 1) * QT)
            units.append(
                (
                    lambda rows=rows, lanes=lanes: q_ref[rows, lanes],
                    lambda head=head: keys[head],
                    lambda head=head: values[head],
                    lambda sums, top, at=(head, rows, lanes): done(sums, top, *at),
                )
            )
    return units


def load0(kv_ref, keys, values):
    for head in range(4):
        keys[head, :HD] = kv_ref[head * HD : (head + 1) * HD, :]
        values[head, :HD] = kv_ref[(4 + head) * HD : (5 + head) * HD, :]
        finish_keys(keys.at[head], values.at[head])


def own_half_kernel(q_ref, kv_ref, out_ref, keys, values):
    load0(kv_ref, keys, values)

    def done(sums, top, head, rows, lanes):
        turned = jnp.where(iota((QT, 64), 1) == HD + 1, top, sums).T
        out_ref[head, :, lanes] = turned

    attend(units0(q_ref, keys, values, done))


def other_half_kernel(*refs):
    (q_ref, kv_ref, half_ref), sources = refs[:3], refs[3:7]
    out_ref, targets, (keys, values, sems) = refs[7], refs[8:12], refs[12:]
    copies = started(
        [
            pltpu.make_async_copy(source, target, sems.at[i])
            for i, (source, target) in enumerate(zip(sources, targets))
        ]
    )
    load0(kv_ref, keys, values)

    def done(sums, top, head, rows, lanes):
        mine = jnp.where(iota((QT, 64), 1) == HD + 1, top, sums).T
        before = half_ref[head, :, lanes]
        top_mine, top_before = mine[HD + 1 : HD + 2], before[HD + 1 : HD + 2]
        top = jnp.maximum(top_mine, top_before)
        total = mine * jnp.exp2(top_mine - top) + before * jnp.exp2(top_before - top)
        out_ref[rows, lanes] = (total[:HD] / jnp.maximum(total[HD : HD + 1], 1e-30)).astype(BF)

    attend(units0(q_ref, keys, values, done))
    finish(copies)


def pack_kernel(*refs):
    got, (far_hbm, farther_hbm, far, sems) = refs[:4], refs[4:]
    for s in range(4):
        far[:, s * 256 : (s + 1) * 256] = got[s][: 2 * HD, 512:768]
        far[:, 1024 + s * 128 : 1024 + (s + 1) * 128] = got[s][: 2 * HD, 768:]
    finish(
        started(
            [
                pltpu.make_async_copy(far, far_hbm, sems.at[0]),
                pltpu.make_async_copy(far.at[:, pl.ds(1024, 512)], farther_hbm, sems.at[1]),
            ]
        )
    )


def loader(keys, values):
    def load(at, block):
        width = block.shape[1]
        keys[:HD, at : at + width] = block[:HD]
        values[:HD, at : at + width] = block[HD:]

    return load


def joined_unit(got, outs, keys, values, parts):
    def query():
        blocks = [got[s][2 * HD :, lanes] for s, lanes in parts]
        return blocks[0] if len(blocks) == 1 else jnp.concatenate(blocks, axis=1)

    def done(sums, top):
        result, at = divided(sums), 0
        for s, lanes in parts:
            width = lanes.stop - lanes.start
            outs[s][:, lanes] = result[:, at : at + width]
            at += width

    return (query, lambda: keys[...], lambda: values[...], done)


def attend1_kernel(*refs):
    got, outs, (keys, values) = refs[:4], refs[4:8], refs[8:]
    load = loader(keys, values)
    for s in range(4):
        load(s * 512, got[s][: 2 * HD, :512])
    finish_keys(keys, values)
    attend(
        [
            joined_unit(got, outs, keys, values, [(s, slice(t * QT, (t + 1) * QT))])
            for s in range(4)
            for t in range(512 // QT)
        ]
    )


def attend23_kernel(*refs):
    got, (x4, x8, x12), first = refs[:4], refs[4:7], refs[7:11]
    outs, (keys, values, sent, sems) = refs[11:15], refs[15:]
    two, three = (keys.at[0], values.at[0]), (keys.at[1], values.at[1])
    for s in range(4):
        loader(*two)(s * 256, got[s][: 2 * HD, 512:768])
        loader(*three)(s * 128, got[s][: 2 * HD, 768:])
    loader(*two)(1024, x4[:, :1024])
    loader(*three)(512, x4[:, 1024:])
    loader(*three)(1024, x8[...])
    loader(*three)(1536, x12[...])
    finish_keys(*two)
    finish_keys(*three)
    made = [outs[0]] + [sent.at[m] for m in range(3)]
    for s in range(4):
        made[s][:, :512] = first[s][...]
    units = [joined_unit(got, made, *two, [(s, slice(512, 768))]) for s in range(4)]
    for s in (0, 2):
        lanes = slice(768, 896)
        units.append(joined_unit(got, made, *three, [(s, lanes), (s + 1, lanes)]))
    attend(units)
    finish(
        started([pltpu.make_async_copy(made[m], outs[m], sems.at[m - 1]) for m in range(1, 4)])
    )


def mlp_kernel(
    off_ref,
    me_ref,
    slots,
    a0_ref,
    aa_ref,
    ab_ref,
    ac_ref,
    ad_ref,
    gain_ref,
    out_weight,
    up,
    down,
    out_hbm,
    attn,
    wide,
    out,
    out_sems,
):
    part = 768
    parts = FF // part
    attn[: 4 * HD, :] = a0_ref[...]
    attn[4 * HD :, :] = jnp.zeros((12 * HD, SLOTS), BF)

    def lanes(rank):
        return pl.ds(pl.multiple_of(rank * OWNERS, OWNERS), OWNERS)

    for m, ref in enumerate((aa_ref, ab_ref, ac_ref, ad_ref)):
        place = lax.bitwise_xor(me_ref[0] % 4, m)
        for group, start, count in GROUPS:
            head = 4 * group + place
            rows = pl.ds(pl.multiple_of(head * HD, 16), HD)
            for i in range(count):
                attn[rows, lanes(off_ref[head] + 2**group * i)] = ref[
                    :, start + i * 128 : start + (i + 1) * 128
                ]

    for t in range(4):
        mixed = lax.dot_general(
            attn[:, t * 256 : (t + 1) * 256], out_weight[...], TN, preferred_element_type=F32
        )
        for i in range(2):
            for c in range(D // 128):
                wide[c, pl.ds(2 * t + i, OWNERS, stride=CAP), :] = mixed[
                    i * OWNERS : (i + 1) * OWNERS, c * 128 : (c + 1) * 128
                ]
    gain = row_of(gain_ref)
    tile = 512

    def written(t):
        span = pl.ds(pl.multiple_of(t * tile, tile), tile)
        return pltpu.make_async_copy(out.at[span], out_hbm.at[0, span], out_sems.at[t])

    def step(t, carry):
        span = pl.ds(pl.multiple_of(t * tile, tile), tile)
        rows = slots[span, :].astype(F32)
        held = rows[:, :1] < LIMIT
        mixed = jnp.concatenate([wide[c, span, :] for c in range(D // 128)], axis=1)
        hidden = jnp.where(held, rows, 0.0) + mixed
        centred, scale = normalise(hidden)
        normed = (centred * scale * gain).astype(BF)

        def raised(f):
            return jnp.dot(normed, up[:, f * part : (f + 1) * part], preferred_element_type=F32)

        final, act = hidden, raised(0)
        for f in range(parts):
            following = raised(f + 1) if f + 1 < parts else None
            final = final + jnp.dot(
                jax.nn.gelu(act).astype(BF),
                down[f * part : (f + 1) * part, :],
                preferred_element_type=F32,
            )
            act = following
        out[span, :] = jnp.where(held, final, 0.0).astype(BF)
        written(t).start()
        return carry

    lax.fori_loop(0, SLOTS // tile, step, 0)
    finish([written(t) for t in range(SLOTS // tile)])


def grad_kernel(
    dest_ref, feats_hbm, gain_ref, weight_hbm, back_hbm, out_hbm, feats, weight, back, out, sems
):
    loads = started(
        [
            pltpu.make_async_copy(back_hbm, back, sems.at[6]),
            pltpu.make_async_copy(weight_hbm, weight, sems.at[0]),
            pltpu.make_async_copy(feats_hbm, feats, sems.at[1]),
        ]
    )
    dest = dest_ref[...]
    slot = (dest * CAP + rank_of(dest)).astype(F32)
    slot = jnp.broadcast_to(slot, (128, TILES)).T[:, :1].astype(jnp.int32)
    gain = row_of(gain_ref)
    copies = []
    for t in range(2):
        span = slice(t * 256, (t + 1) * 256)
        place = (iota((256, SLOTS), 1) == slot[span]).astype(F32).astype(BF)
        if t == 0:
            loads[0].wait()
        rows = jnp.dot(place, back[...], preferred_element_type=F32).astype(BF)
        if t == 0:
            loads[1].wait()
        grad = lax.dot_general(rows, weight[...], NT, preferred_element_type=F32) * gain
        if t == 0:
            loads[2].wait()
        centred, scale = normalise(feats[span, :].astype(F32))
        unit = centred * scale
        along = jnp.mean(grad * unit, axis=-1, keepdims=True)
        level = jnp.mean(grad, axis=-1, keepdims=True)
        out[span, :] = (scale * (grad - level - unit * along)).astype(BF)
        part = pl.ds(t * 256, 256)
        copies += started([pltpu.make_async_copy(out.at[part], out_hbm.at[part], sems.at[2 + t])])
    finish(copies)


def per_device(
    tile_feats,
    tile_gain,
    proj_weight,
    proj_bias,
    dest,
    slot_gain,
    qkv_weight,
    out_weight,
    mlp_gain,
    up_weight,
    down_weight,
    offsets,
    slot_grad,
):
    sds = jax.ShapeDtypeStruct

    def in_hbm(array):
        return pltpu.with_memory_space_constraint(array, pltpu.HBM)

    def in_vmem(array):
        return pltpu.with_memory_space_constraint(array, pltpu.VMEM)

    everyone = ("tile", "seq")
    me = lax.axis_index("seq").astype(jnp.int32).reshape(1)
    dest = dest.reshape(1, TILES)
    order = lax.optimization_barrier

    outgoing = call(
        embed_kernel,
        sds((SLOTS, D), BF),
        (pltpu.VMEM((TILES, DT), BF), pltpu.VMEM((DT, D), BF), pltpu.VMEM((SLOTS, D), BF), DMA((4,))),
        VMEM,
        2 * 10**9,
        "embed_tiles",
        [VM, HBM, VM, HBM, VM],
        HBM,
    )(
        in_hbm(dest),
        in_hbm(tile_feats),
        in_hbm(tile_gain),
        in_hbm(proj_weight),
        in_hbm(proj_bias),
    )
    outgoing, qkv_weight = order((outgoing, qkv_weight))
    slots = lax.all_to_all(outgoing, everyone, split_axis=0, concat_axis=0, tiled=True)
    turned = call(turn_kernel, sds((3 * D, D), BF), (), VMEM, 8 * 10**9, "turn_qkv_weight")(
        qkv_weight
    )
    slots, turned, slot_grad = order((slots, turned, slot_grad))
    turned = in_hbm(turned)
    returned = lax.all_to_all(slot_grad[0], everyone, split_axis=0, concat_axis=0, tiled=True)

    part = sds((3 * HD, TAKEN), BF)
    kv0_shape = sds((8 * HD, SLOTS), BF)
    q0, kv0, *parts, kv0_sent = call(
        qkv_kernel,
        (sds((4 * HD, SLOTS), BF), kv0_shape, part, part, part, part, kv0_shape),
        (
            pltpu.VMEM((D // 128, SLOTS, 128), F32),
            pltpu.VMEM((3 * D, SLOTS), BF),
            pltpu.VMEM((3 * D, D), BF),
            pltpu.VMEM((3, 3 * HD, TAKEN), BF),
            DMA((6,)),
        ),
        VMEM,
        4 * 10**9,
        "make_qkv",
        [SM, SM, VM, VM, HBM],
        (VM, VM, VM, HBM, HBM, HBM, HBM),
    )(offsets, me, slots, in_hbm(slot_gain), turned)

    def send(array, m):
        return lax.ppermute(array, "seq", [(i, i ^ m) for i in range(N_SEQ)])

    one_head = (pltpu.VMEM((64, KEYS), BF), pltpu.VMEM((64, KEYS), BF))
    two_heads = (pltpu.VMEM((2, 64, KEYS), BF), pltpu.VMEM((2, 64, KEYS), BF))
    four_heads = (pltpu.VMEM((4, 64, SLOTS), BF), pltpu.VMEM((4, 64, SLOTS), BF))
    parts = [parts[0]] + [send(parts[m], m) for m in range(1, 4)]
    other = send(kv0_sent, 1)
    half = call(
        own_half_kernel, sds((4, 64, SLOTS), F32), four_heads, VMEM, 8 * 10**9, "attend_own_half"
    )(q0, kv0)
    returned, half = order((returned, half))
    tile_grad = call(
        grad_kernel,
        sds((TILES, DT), BF),
        (
            pltpu.VMEM((TILES, DT), BF),
            pltpu.VMEM((DT, D), BF),
            pltpu.VMEM((SLOTS, D), BF),
            pltpu.VMEM((TILES, DT), BF),
            DMA((7,)),
        ),
        VMEM,
        4 * 10**9,
        "tile_cotangent",
        [VM, HBM, VM, HBM, HBM],
        HBM,
    )(
        in_hbm(dest),
        in_hbm(tile_feats),
        in_hbm(tile_gain),
        in_hbm(proj_weight),
        in_hbm(returned),
    )
    tile_grad, half, *parts = order((tile_grad, half, *parts))
    parts = [in_vmem(array) for array in parts]
    far, farther = call(
        pack_kernel,
        (sds((2 * HD, 1536), BF), sds((2 * HD, 512), BF)),
        (pltpu.VMEM((2 * HD, 1536), BF), DMA((2,))),
        VMEM,
        10**9,
        "pack_far_keys",
        None,
        (HBM, HBM),
    )(*parts)
    x12, x8, x4 = send(farther, 12), send(farther, 8), send(far, 4)
    result = sds((HD, TAKEN), BF)
    first = call(
        attend1_kernel, (sds((HD, 512), BF),) * 4, one_head, VMEM, 8 * 10**9, "attend_group1"
    )(*parts)
    x4, x8, x12, *first = order((x4, x8, x12, *first))
    rest = call(
        attend23_kernel,
        (result,) * 4,
        two_heads + (pltpu.VMEM((3, HD, TAKEN), BF), DMA((3,))),
        VMEM,
        6 * 10**9,
        "attend_groups23",
        None,
        (VM, HBM, HBM, HBM),
    )(*parts, x4, x8, x12, *first)
    other, half, *rest = order((other, half, *rest))
    rest = [rest[0]] + [send(rest[m], m) for m in range(1, 4)]
    a0, *held = call(
        other_half_kernel,
        (
            sds((4 * HD, SLOTS), BF),
            sds((SLOTS, D), BF),
            sds((D, D), BF),
            sds((D, FF), BF),
            sds((FF, D), BF),
        ),
        four_heads + (DMA((4,)),),
        VMEM,
        8 * 10**9,
        "attend_other_half",
        [VM] * 3 + [HBM] * 4,
    )(
        in_vmem(q0),
        in_vmem(other),
        in_vmem(half),
        *(in_hbm(array) for array in (slots, out_weight, up_weight, down_weight)),
    )
    a0, *rest = order((a0, *rest))
    slots, out_weight, up_weight, down_weight = (in_vmem(array) for array in held)

    slide_states = call(
        mlp_kernel,
        sds((1, SLOTS, D), BF),
        (
            pltpu.VMEM((D, SLOTS), BF),
            pltpu.VMEM((D // 128, SLOTS, 128), F32),
            pltpu.VMEM((SLOTS, D), BF),
            DMA((2,)),
        ),
        40,
        11 * 10**9,
        "out_and_mlp",
        [SM, SM] + [VM] * 10,
        HBM,
    )(offsets, me, slots, a0, *rest, in_hbm(mlp_gain), out_weight, up_weight, down_weight)
    return (slide_states, tile_grad)


def solution(mesh):
    return jax.shard_map(
        per_device,
        mesh=mesh,
        in_specs=(
            P(("tile", "seq"), None),
            P(),
            P(),
            P(),
            P(("tile", "seq"), None),
            P(),
            P(),
            P(),
            P(),
            P(),
            P(),
            P(),
            P("tile", "seq", None),
        ),
        out_specs=(P("tile", "seq", None), P(("tile", "seq"), None)),
        check_vma=False,
    )
```

```python
import math

import jax
import jax.numpy as jnp
from jax import lax
from jax.experimental import pallas as pl
from jax.experimental.pallas import tpu as pltpu
from jax.sharding import PartitionSpec as P

DT = 1536
D = 768
HEADS = 16
FF = 3072
HD = 48
TILES = 512
CAP = 8
OWNERS = 128
SLOTS = 1024
KEYS = 2048
N_SEQ = 16
EPS = 1e-05
MIB = 2**20
VMEM = 32

EMPTY = 3e38
LIMIT = 1e37
MASKED = -1e30
SCALE = HD**-0.5 * math.log2(math.e)

BF = jnp.bfloat16
F32 = jnp.float32
NT = (((1,), (1,)), ((), ()))
TN = (((0,), (0,)), ((), ()))


def iota(shape, axis):
    return lax.broadcasted_iota(jnp.int32, shape, axis)


def normalise(values):
    mean = jnp.mean(values, axis=-1, keepdims=True)
    centred = values - mean
    spread = jnp.mean(centred * centred, axis=-1, keepdims=True)
    return centred, lax.rsqrt(spread + EPS)


def call(kernel, outs, scratch, vmem, flops, name, in_specs=None, out_specs=None):
    specs = {} if in_specs is None else {"in_specs": in_specs}
    if out_specs is not None:
        specs["out_specs"] = out_specs
    return pl.pallas_call(
        kernel,
        out_shape=outs,
        **specs,
        scratch_shapes=scratch,
        name=name,
        compiler_params=pltpu.CompilerParams(vmem_limit_bytes=vmem * MIB),
        cost_estimate=pl.CostEstimate(flops=flops, bytes_accessed=8 * MIB, transcendentals=0),
    )


VM = pl.BlockSpec(memory_space=pltpu.VMEM)
SM = pl.BlockSpec(memory_space=pltpu.SMEM)
HBM = pl.BlockSpec(memory_space=pltpu.HBM)
DMA = pltpu.SemaphoreType.DMA


def started(copies):
    for copy in copies:
        copy.start()
    return copies


def finish(copies):
    for copy in copies:
        copy.wait()


GROUPS = ((1, 0, 4), (2, 512, 2), (3, 768, 1))
TAKEN = 896


def row_of(ref):
    return ref[...].reshape(1, ref.shape[0])


def rank_of(dest):
    hot = (iota((OWNERS, TILES), 0) == dest).astype(F32)
    earlier = (iota((TILES, TILES), 0) < iota((TILES, TILES), 1)).astype(F32).astype(BF)
    before = jnp.dot(hot.astype(BF), earlier, preferred_element_type=F32)
    return jnp.sum(before * hot, axis=0, keepdims=True).astype(jnp.int32)


def embed_kernel(
    dest_ref, feats_hbm, gain_ref, weight_hbm, bias_ref, out_hbm, feats, weight, out, sems
):
    loads = started(
        [
            pltpu.make_async_copy(feats_hbm, feats, sems.at[0]),
            pltpu.make_async_copy(weight_hbm, weight, sems.at[1]),
        ]
    )
    dest = dest_ref[...]
    place = (iota((SLOTS, TILES), 0) == dest * CAP + rank_of(dest)).astype(F32)
    taken = jnp.max(place, axis=1, keepdims=True)
    place = place.astype(BF)
    gain, bias = row_of(gain_ref), row_of(bias_ref)
    loads[0].wait()
    normed = []
    for t in range(2):
        centred, scale = normalise(feats[t * 256 : (t + 1) * 256, :].astype(F32))
        normed.append((centred * scale * gain).astype(BF))
    loads[1].wait()
    emb = [
        (jnp.dot(part, weight[...], preferred_element_type=F32) + bias).astype(BF)
        for part in normed
    ]
    emb = jnp.concatenate(emb, axis=0)
    copies = []
    for t in range(2):
        span = slice(t * 512, (t + 1) * 512)
        rows = jnp.dot(place[span], emb, preferred_element_type=F32)
        out[span, :] = jnp.where(taken[span] > 0, rows, EMPTY).astype(BF)
        part = pl.ds(t * 512, 512)
        copies += started([pltpu.make_async_copy(out.at[part], out_hbm.at[part], sems.at[2 + t])])
    finish(copies)


def turn_kernel(weight_ref, out_ref):
    for i in range(6):
        cols = slice(i * 384, (i + 1) * 384)
        out_ref[cols, :] = weight_ref[:, cols].T


def qkv_kernel(
    off_ref,
    me_ref,
    slots_ref,
    gain_ref,
    weight_hbm,
    q0_ref,
    kv0_ref,
    sa_ref,
    sb_hbm,
    sc_hbm,
    sd_hbm,
    kv0_hbm,
    q0_hbm,
    wide,
    mixed,
    weight,
    sent,
    sems,
):
    loads = started([pltpu.make_async_copy(weight_hbm, weight, sems.at[0])])
    for c in range(D // 128):
        wide[c] = slots_ref[:, c * 128 : (c + 1) * 128].astype(F32)
    gain = row_of(gain_ref)

    def prepared(block):
        flags, normed = [], []
        for r in (2 * block, 2 * block + 1):
            rows = jnp.concatenate(
                [wide[c, pl.ds(r, OWNERS, stride=CAP), :] for c in range(D // 128)], axis=1
            )
            held = rows[:, :1] < LIMIT
            flags.append(jnp.broadcast_to(held.astype(F32), (OWNERS, 128)).T[:1])
            centred, scale = normalise(jnp.where(held, rows, 0.0))
            normed.append((centred * scale * gain).astype(BF))
        return jnp.concatenate(flags, axis=1) > 0, jnp.concatenate(normed, axis=0)

    state = prepared(0)
    finish(loads)
    for block in range(4):
        held, normed = state
        if block < 3:
            state = prepared(block + 1)
        lanes = slice(block * 256, (block + 1) * 256)
        for part in range(3):
            rows = slice(part * D, (part + 1) * D)
            made = lax.dot_general(weight[rows, :], normed, NT, preferred_element_type=F32)
            if part == 0:
                made = made * SCALE
            if part == 1:
                made = jnp.where(held, made, EMPTY)
            mixed[rows, lanes] = made.astype(BF)
    copies = started(
        [
            pltpu.make_async_copy(mixed.at[pl.ds(D, 4 * HD)], kv0_hbm.at[pl.ds(0, 4 * HD)], sems.at[1]),
            pltpu.make_async_copy(
                mixed.at[pl.ds(2 * D, 4 * HD)], kv0_hbm.at[pl.ds(4 * HD, 4 * HD)], sems.at[2]
            ),
            pltpu.make_async_copy(mixed.at[pl.ds(0, 4 * HD)], q0_hbm, sems.at[6]),
        ]
    )

    def piece(part, head, rank):
        lanes = pl.ds(pl.multiple_of(rank * OWNERS, OWNERS), OWNERS)
        return mixed[pl.ds(pl.multiple_of(part * D + head * HD, 16), HD), lanes]

    for m in (1, 2, 3, 0):
        ref = sent.at[m - 1] if m else sa_ref
        place = lax.bitwise_xor(me_ref[0] % 4, m)
        for group, start, count in GROUPS:
            head = 4 * group + place
            for row, part in enumerate((1, 2, 0)):
                for i in range(count):
                    ref[row * HD : (row + 1) * HD, start + i * 128 : start + (i + 1) * 128] = piece(
                        part, head, off_ref[head] + 2**group * i
                    )
        if m:
            target = (sb_hbm, sc_hbm, sd_hbm)[m - 1]
            copies += started([pltpu.make_async_copy(ref, target, sems.at[2 + m])])
    q0_ref[...] = mixed[0 : 4 * HD, :]
    kv0_ref[0 : 4 * HD, :] = mixed[D : D + 4 * HD, :]
    kv0_ref[4 * HD :, :] = mixed[2 * D : 2 * D + 4 * HD, :]
    finish(copies)


def finish_keys(keys, values):
    width = keys.shape[1]
    top = iota((16, width), 0) == 0
    empty = keys[0:1, :].astype(F32) > LIMIT
    keys[HD:, :] = jnp.where(top & empty, MASKED, 0.0).astype(BF)
    keys[:HD, :] = jnp.where(empty, 0.0, keys[:HD, :].astype(F32)).astype(BF)
    values[HD:, :] = jnp.where(top, 1.0, 0.0).astype(BF)


def with_ones(query):
    width = query.shape[1]
    ones = jnp.where(iota((16, width), 0) == 0, 1.0, 0.0).astype(BF)
    return jnp.concatenate([query, ones], axis=0)


def attend(units):
    def score(unit):
        return jnp.dot(with_ones(unit[0]()).T, unit[1](), preferred_element_type=F32)

    scores = score(units[0])
    for i, unit in enumerate(units):
        top = jnp.max(scores, axis=1, keepdims=True)
        later = score(units[i + 1]) if i + 1 < len(units) else None
        weights = jnp.exp2(scores - top).astype(BF)
        sums = lax.dot_general(weights, unit[2](), NT, preferred_element_type=F32)
        unit[3](sums, top)
        scores = later


def divided(sums):
    turned = sums.T
    return (turned[:HD] / jnp.maximum(turned[HD : HD + 1], 1e-30)).astype(BF)


QT = 256


def units0(q_ref, keys, values, done):
    units = []
    for head in range(4):
        for t in range(SLOTS // QT):
            rows, lanes = slice(head * HD, (head + 1) * HD), slice(t * QT, (t + 1) * QT)
            units.append(
                (
                    lambda rows=rows, lanes=lanes: q_ref[rows, lanes],
                    lambda head=head: keys[head],
                    lambda head=head: values[head],
                    lambda sums, top, at=(head, rows, lanes): done(sums, top, *at),
                )
            )
    return units


def load0(kv_ref, keys, values):
    for head in range(4):
        keys[head, :HD] = kv_ref[head * HD : (head + 1) * HD, :]
        values[head, :HD] = kv_ref[(4 + head) * HD : (5 + head) * HD, :]
        finish_keys(keys.at[head], values.at[head])


def own_half_kernel(
    q_ref,
    kv_ref,
    feats_hbm,
    weight_hbm,
    out_hbm,
    feats_ref,
    weight_ref,
    keys,
    values,
    out,
    sems,
):
    copies = started(
        [
            pltpu.make_async_copy(feats_hbm, feats_ref, sems.at[4]),
            pltpu.make_async_copy(weight_hbm, weight_ref, sems.at[5]),
        ]
    )
    load0(kv_ref, keys, values)

    def done(sums, top, head, rows, lanes):
        turned = jnp.where(iota((QT, 64), 1) == HD + 1, top, sums).T
        out[head, :, lanes] = turned
        if lanes.stop == SLOTS:
            copies.append(pltpu.make_async_copy(out.at[head], out_hbm.at[head], sems.at[head]))
            copies[-1].start()

    attend(units0(q_ref, keys, values, done))
    finish(copies)


def other_half_kernel(*refs):
    (q_hbm, kv_ref, half_hbm), sources = refs[:3], refs[3:7]
    out_ref, targets, (keys, values, q_ref, half_ref, sems) = refs[7], refs[8:12], refs[12:]
    needed = started(
        [
            pltpu.make_async_copy(q_hbm, q_ref, sems.at[4]),
            pltpu.make_async_copy(half_hbm, half_ref, sems.at[5]),
        ]
    )
    copies = started(
        [
            pltpu.make_async_copy(source, target, sems.at[i])
            for i, (source, target) in enumerate(zip(sources, targets))
        ]
    )
    load0(kv_ref, keys, values)
    finish(needed)

    def done(sums, top, head, rows, lanes):
        mine = jnp.where(iota((QT, 64), 1) == HD + 1, top, sums).T
        before = half_ref[head, :, lanes]
        top_mine, top_before = mine[HD + 1 : HD + 2], before[HD + 1 : HD + 2]
        top = jnp.maximum(top_mine, top_before)
        total = mine * jnp.exp2(top_mine - top) + before * jnp.exp2(top_before - top)
        out_ref[rows, lanes] = (total[:HD] / jnp.maximum(total[HD : HD + 1], 1e-30)).astype(BF)

    attend(units0(q_ref, keys, values, done))
    finish(copies)


def pack_kernel(*refs):
    got, (far_hbm, farther_hbm, far, sems) = refs[:4], refs[4:]
    for s in range(4):
        far[:, s * 256 : (s + 1) * 256] = got[s][: 2 * HD, 512:768]
        far[:, 1024 + s * 128 : 1024 + (s + 1) * 128] = got[s][: 2 * HD, 768:]
    finish(
        started(
            [
                pltpu.make_async_copy(far, far_hbm, sems.at[0]),
                pltpu.make_async_copy(far.at[:, pl.ds(1024, 512)], farther_hbm, sems.at[1]),
            ]
        )
    )


def loader(keys, values):
    def load(at, block):
        width = block.shape[1]
        keys[:HD, at : at + width] = block[:HD]
        values[:HD, at : at + width] = block[HD:]

    return load


def joined_unit(got, outs, keys, values, parts):
    def query():
        blocks = [got[s][2 * HD :, lanes] for s, lanes in parts]
        return blocks[0] if len(blocks) == 1 else jnp.concatenate(blocks, axis=1)

    def done(sums, top):
        result, at = divided(sums), 0
        for s, lanes in parts:
            width = lanes.stop - lanes.start
            outs[s][:, lanes] = result[:, at : at + width]
            at += width

    return (query, lambda: keys[...], lambda: values[...], done)


def attend1_kernel(*refs):
    got, outs, (keys, values) = refs[:4], refs[4:8], refs[8:]
    load = loader(keys, values)
    for s in range(4):
        load(s * 512, got[s][: 2 * HD, :512])
    finish_keys(keys, values)
    attend(
        [
            joined_unit(got, outs, keys, values, [(s, slice(t * QT, (t + 1) * QT))])
            for s in range(4)
            for t in range(512 // QT)
        ]
    )


def attend23_kernel(*refs):
    got, (x4, x8, x12), first = refs[:4], refs[4:7], refs[7:11]
    outs, (keys, values, sent, sems) = refs[11:15], refs[15:]
    two, three = (keys.at[0], values.at[0]), (keys.at[1], values.at[1])
    for s in range(4):
        loader(*two)(s * 256, got[s][: 2 * HD, 512:768])
        loader(*three)(s * 128, got[s][: 2 * HD, 768:])
    loader(*two)(1024, x4[:, :1024])
    loader(*three)(512, x4[:, 1024:])
    loader(*three)(1024, x8[...])
    loader(*three)(1536, x12[...])
    finish_keys(*two)
    finish_keys(*three)
    made = [outs[0]] + [sent.at[m] for m in range(3)]
    for s in range(4):
        made[s][:, :512] = first[s][...]
    units = [joined_unit(got, made, *two, [(s, slice(512, 768))]) for s in range(4)]
    for s in (0, 2):
        lanes = slice(768, 896)
        units.append(joined_unit(got, made, *three, [(s, lanes), (s + 1, lanes)]))
    attend(units)
    finish(
        started([pltpu.make_async_copy(made[m], outs[m], sems.at[m - 1]) for m in range(1, 4)])
    )


def mlp_kernel(
    off_ref,
    me_ref,
    slots,
    a0_ref,
    aa_ref,
    ab_ref,
    ac_ref,
    ad_ref,
    gain_ref,
    out_weight,
    up,
    down,
    out_hbm,
    attn,
    wide,
    out,
    out_sems,
):
    part = 768
    parts = FF // part
    attn[: 4 * HD, :] = a0_ref[...]
    attn[4 * HD :, :] = jnp.zeros((12 * HD, SLOTS), BF)

    def lanes(rank):
        return pl.ds(pl.multiple_of(rank * OWNERS, OWNERS), OWNERS)

    for m, ref in enumerate((aa_ref, ab_ref, ac_ref, ad_ref)):
        place = lax.bitwise_xor(me_ref[0] % 4, m)
        for group, start, count in GROUPS:
            head = 4 * group + place
            rows = pl.ds(pl.multiple_of(head * HD, 16), HD)
            for i in range(count):
                attn[rows, lanes(off_ref[head] + 2**group * i)] = ref[
                    :, start + i * 128 : start + (i + 1) * 128
                ]

    for t in range(4):
        mixed = lax.dot_general(
            attn[:, t * 256 : (t + 1) * 256], out_weight[...], TN, preferred_element_type=F32
        )
        for i in range(2):
            for c in range(D // 128):
                wide[c, pl.ds(2 * t + i, OWNERS, stride=CAP), :] = mixed[
                    i * OWNERS : (i + 1) * OWNERS, c * 128 : (c + 1) * 128
                ]
    gain = row_of(gain_ref)
    tile = 512

    def written(t):
        span = pl.ds(pl.multiple_of(t * tile, tile), tile)
        return pltpu.make_async_copy(out.at[span], out_hbm.at[0, span], out_sems.at[t])

    def step(t, carry):
        span = pl.ds(pl.multiple_of(t * tile, tile), tile)
        rows = slots[span, :].astype(F32)
        held = rows[:, :1] < LIMIT
        mixed = jnp.concatenate([wide[c, span, :] for c in range(D // 128)], axis=1)
        hidden = jnp.where(held, rows, 0.0) + mixed
        centred, scale = normalise(hidden)
        normed = (centred * scale * gain).astype(BF)

        def raised(f):
            return jnp.dot(normed, up[:, f * part : (f + 1) * part], preferred_element_type=F32)

        final, act = hidden, raised(0)
        for f in range(parts):
            following = raised(f + 1) if f + 1 < parts else None
            final = final + jnp.dot(
                jax.nn.gelu(act).astype(BF),
                down[f * part : (f + 1) * part, :],
                preferred_element_type=F32,
            )
            act = following
        out[span, :] = jnp.where(held, final, 0.0).astype(BF)
        written(t).start()
        return carry

    lax.fori_loop(0, SLOTS // tile, step, 0)
    finish([written(t) for t in range(SLOTS // tile)])


def grad_kernel(
    dest_ref, feats, gain_ref, weight, back_hbm, out_hbm, back, out, sems
):
    loads = started(
        [
            pltpu.make_async_copy(back_hbm, back, sems.at[0]),
        ]
    )
    dest = dest_ref[...]
    slot = (dest * CAP + rank_of(dest)).astype(F32)
    slot = jnp.broadcast_to(slot, (128, TILES)).T[:, :1].astype(jnp.int32)
    gain = row_of(gain_ref)
    copies = []
    for t in range(2):
        span = slice(t * 256, (t + 1) * 256)
        place = (iota((256, SLOTS), 1) == slot[span]).astype(F32).astype(BF)
        if t == 0:
            loads[0].wait()
        rows = jnp.dot(place, back[...], preferred_element_type=F32).astype(BF)
        grad = lax.dot_general(rows, weight[...], NT, preferred_element_type=F32) * gain
        centred, scale = normalise(feats[span, :].astype(F32))
        unit = centred * scale
        along = jnp.mean(grad * unit, axis=-1, keepdims=True)
        level = jnp.mean(grad, axis=-1, keepdims=True)
        out[span, :] = (scale * (grad - level - unit * along)).astype(BF)
        part = pl.ds(t * 256, 256)
        copies += started([pltpu.make_async_copy(out.at[part], out_hbm.at[part], sems.at[1 + t])])
    finish(copies)


def per_device(
    tile_feats,
    tile_gain,
    proj_weight,
    proj_bias,
    dest,
    slot_gain,
    qkv_weight,
    out_weight,
    mlp_gain,
    up_weight,
    down_weight,
    offsets,
    slot_grad,
):
    sds = jax.ShapeDtypeStruct

    def in_hbm(array):
        return pltpu.with_memory_space_constraint(array, pltpu.HBM)

    def in_vmem(array):
        return pltpu.with_memory_space_constraint(array, pltpu.VMEM)

    everyone = ("tile", "seq")
    me = lax.axis_index("seq").astype(jnp.int32).reshape(1)
    dest = dest.reshape(1, TILES)
    order = lax.optimization_barrier

    outgoing = call(
        embed_kernel,
        sds((SLOTS, D), BF),
        (pltpu.VMEM((TILES, DT), BF), pltpu.VMEM((DT, D), BF), pltpu.VMEM((SLOTS, D), BF), DMA((4,))),
        VMEM,
        2 * 10**9,
        "embed_tiles",
        [VM, HBM, VM, HBM, VM],
        HBM,
    )(
        in_hbm(dest),
        in_hbm(tile_feats),
        in_hbm(tile_gain),
        in_hbm(proj_weight),
        in_hbm(proj_bias),
    )
    outgoing, qkv_weight = order((outgoing, qkv_weight))
    slots = lax.all_to_all(outgoing, everyone, split_axis=0, concat_axis=0, tiled=True)
    turned = call(turn_kernel, sds((3 * D, D), BF), (), VMEM, 8 * 10**9, "turn_qkv_weight")(
        qkv_weight
    )
    slots, turned, slot_grad = order((slots, turned, slot_grad))
    turned = in_hbm(turned)
    returned = lax.all_to_all(slot_grad[0], everyone, split_axis=0, concat_axis=0, tiled=True)

    part = sds((3 * HD, TAKEN), BF)
    kv0_shape = sds((8 * HD, SLOTS), BF)
    q0, kv0, *parts, kv0_sent, q0_kept = call(
        qkv_kernel,
        (
            sds((4 * HD, SLOTS), BF),
            kv0_shape,
            part,
            part,
            part,
            part,
            kv0_shape,
            pltpu.HBM((4 * HD, SLOTS), BF),
        ),
        (
            pltpu.VMEM((D // 128, SLOTS, 128), F32),
            pltpu.VMEM((3 * D, SLOTS), BF),
            pltpu.VMEM((3 * D, D), BF),
            pltpu.VMEM((3, 3 * HD, TAKEN), BF),
            DMA((7,)),
        ),
        VMEM,
        4 * 10**9,
        "make_qkv",
        [SM, SM, VM, VM, HBM],
        (VM, VM, VM, HBM, HBM, HBM, HBM, HBM),
    )(offsets, me, slots, in_hbm(slot_gain), turned)

    def send(array, m):
        return lax.ppermute(array, "seq", [(i, i ^ m) for i in range(N_SEQ)])

    one_head = (pltpu.VMEM((64, KEYS), BF), pltpu.VMEM((64, KEYS), BF))
    two_heads = (pltpu.VMEM((2, 64, KEYS), BF), pltpu.VMEM((2, 64, KEYS), BF))
    four_heads = (pltpu.VMEM((4, 64, SLOTS), BF), pltpu.VMEM((4, 64, SLOTS), BF))
    parts = [parts[0]] + [send(parts[m], m) for m in range(1, 4)]
    other = send(kv0_sent, 1)
    half, feats, weight = call(
        own_half_kernel,
        (pltpu.HBM((4, 64, SLOTS), F32), sds((TILES, DT), BF), sds((DT, D), BF)),
        four_heads + (pltpu.VMEM((4, 64, SLOTS), F32), DMA((6,))),
        VMEM,
        8 * 10**9,
        "attend_own_half",
        [VM, VM, HBM, HBM],
        (HBM, VM, VM),
    )(q0, kv0, in_hbm(tile_feats), in_hbm(proj_weight))
    returned, half, feats, weight = order((returned, half, feats, weight))
    tile_grad = call(
        grad_kernel,
        sds((TILES, DT), BF),
        (pltpu.VMEM((SLOTS, D), BF), pltpu.VMEM((TILES, DT), BF), DMA((3,))),
        VMEM,
        4 * 10**9,
        "tile_cotangent",
        [VM, VM, VM, VM, HBM],
        HBM,
    )(in_hbm(dest), in_vmem(feats), in_hbm(tile_gain), in_vmem(weight), in_hbm(returned))
    tile_grad, half, *parts = order((tile_grad, half, *parts))
    parts = [in_vmem(array) for array in parts]
    far, farther = call(
        pack_kernel,
        (sds((2 * HD, 1536), BF), sds((2 * HD, 512), BF)),
        (pltpu.VMEM((2 * HD, 1536), BF), DMA((2,))),
        VMEM,
        10**9,
        "pack_far_keys",
        None,
        (HBM, HBM),
    )(*parts)
    x12, x8, x4 = send(farther, 12), send(farther, 8), send(far, 4)
    result = sds((HD, TAKEN), BF)
    first = call(
        attend1_kernel, (sds((HD, 512), BF),) * 4, one_head, VMEM, 8 * 10**9, "attend_group1"
    )(*parts)
    x4, x8, x12, *first = order((x4, x8, x12, *first))
    rest = call(
        attend23_kernel,
        (result,) * 4,
        two_heads + (pltpu.VMEM((3, HD, TAKEN), BF), DMA((3,))),
        VMEM,
        6 * 10**9,
        "attend_groups23",
        None,
        (VM, HBM, HBM, HBM),
    )(*parts, x4, x8, x12, *first)
    other, half, *rest = order((other, half, *rest))
    rest = [rest[0]] + [send(rest[m], m) for m in range(1, 4)]
    a0, *held = call(
        other_half_kernel,
        (
            sds((4 * HD, SLOTS), BF),
            sds((SLOTS, D), BF),
            sds((D, D), BF),
            sds((D, FF), BF),
            sds((FF, D), BF),
        ),
        four_heads
        + (pltpu.VMEM((4 * HD, SLOTS), BF), pltpu.VMEM((4, 64, SLOTS), F32), DMA((6,))),
        VMEM,
        8 * 10**9,
        "attend_other_half",
        [HBM, VM, HBM] + [HBM] * 4,
    )(
        in_hbm(q0_kept),
        in_vmem(other),
        in_hbm(half),
        *(in_hbm(array) for array in (slots, out_weight, up_weight, down_weight)),
    )
    a0, *rest = order((a0, *rest))
    slots, out_weight, up_weight, down_weight = (in_vmem(array) for array in held)

    slide_states = call(
        mlp_kernel,
        sds((1, SLOTS, D), BF),
        (
            pltpu.VMEM((D, SLOTS), BF),
            pltpu.VMEM((D // 128, SLOTS, 128), F32),
            pltpu.VMEM((SLOTS, D), BF),
            DMA((2,)),
        ),
        40,
        11 * 10**9,
        "out_and_mlp",
        [SM, SM] + [VM] * 10,
        HBM,
    )(offsets, me, slots, a0, *rest, in_hbm(mlp_gain), out_weight, up_weight, down_weight)
    return (slide_states, tile_grad)


def solution(mesh):
    return jax.shard_map(
        per_device,
        mesh=mesh,
        in_specs=(
            P(("tile", "seq"), None),
            P(),
            P(),
            P(),
            P(("tile", "seq"), None),
            P(),
            P(),
            P(),
            P(),
            P(),
            P(),
            P(),
            P("tile", "seq", None),
        ),
        out_specs=(P("tile", "seq", None), P(("tile", "seq"), None)),
        check_vma=False,
    )
```

```python
import math

import jax
import jax.numpy as jnp
from jax import lax
from jax.experimental import pallas as pl
from jax.experimental.pallas import tpu as pltpu
from jax.sharding import PartitionSpec as P

DT = 1536
D = 768
HEADS = 16
FF = 3072
HD = 48
TILES = 512
CAP = 8
OWNERS = 128
SLOTS = 1024
KEYS = 2048
N_SEQ = 16
EPS = 1e-05
MIB = 2**20
VMEM = 32

EMPTY = 3e38
LIMIT = 1e37
MASKED = -1e30
SCALE = HD**-0.5 * math.log2(math.e)

BF = jnp.bfloat16
F32 = jnp.float32
NT = (((1,), (1,)), ((), ()))
TN = (((0,), (0,)), ((), ()))


def iota(shape, axis):
    return lax.broadcasted_iota(jnp.int32, shape, axis)


def normalise(values):
    mean = jnp.mean(values, axis=-1, keepdims=True)
    centred = values - mean
    spread = jnp.mean(centred * centred, axis=-1, keepdims=True)
    return centred, lax.rsqrt(spread + EPS)


def call(kernel, outs, scratch, vmem, flops, name, in_specs=None, out_specs=None):
    specs = {} if in_specs is None else {"in_specs": in_specs}
    if out_specs is not None:
        specs["out_specs"] = out_specs
    return pl.pallas_call(
        kernel,
        out_shape=outs,
        **specs,
        scratch_shapes=scratch,
        name=name,
        compiler_params=pltpu.CompilerParams(vmem_limit_bytes=vmem * MIB),
        cost_estimate=pl.CostEstimate(flops=flops, bytes_accessed=8 * MIB, transcendentals=0),
    )


VM = pl.BlockSpec(memory_space=pltpu.VMEM)
SM = pl.BlockSpec(memory_space=pltpu.SMEM)
HBM = pl.BlockSpec(memory_space=pltpu.HBM)
DMA = pltpu.SemaphoreType.DMA


def started(copies):
    for copy in copies:
        copy.start()
    return copies


def finish(copies):
    for copy in copies:
        copy.wait()


GROUPS = ((1, 0, 4), (2, 512, 2), (3, 768, 1))
TAKEN = 896


def row_of(ref):
    return ref[...].reshape(1, ref.shape[0])


def rank_of(dest):
    hot = (iota((OWNERS, TILES), 0) == dest).astype(F32)
    earlier = (iota((TILES, TILES), 0) < iota((TILES, TILES), 1)).astype(F32).astype(BF)
    before = jnp.dot(hot.astype(BF), earlier, preferred_element_type=F32)
    return jnp.sum(before * hot, axis=0, keepdims=True).astype(jnp.int32)


def embed_kernel(
    dest_ref, feats_hbm, gain_ref, weight_hbm, bias_ref, out_hbm, feats, weight, out, sems
):
    loads = started(
        [
            pltpu.make_async_copy(feats_hbm, feats, sems.at[0]),
            pltpu.make_async_copy(weight_hbm, weight, sems.at[1]),
        ]
    )
    dest = dest_ref[...]
    place = (iota((SLOTS, TILES), 0) == dest * CAP + rank_of(dest)).astype(F32)
    taken = jnp.max(place, axis=1, keepdims=True)
    place = place.astype(BF)
    gain, bias = row_of(gain_ref), row_of(bias_ref)
    loads[0].wait()
    normed = []
    for t in range(2):
        centred, scale = normalise(feats[t * 256 : (t + 1) * 256, :].astype(F32))
        normed.append((centred * scale * gain).astype(BF))
    loads[1].wait()
    emb = [
        (jnp.dot(part, weight[...], preferred_element_type=F32) + bias).astype(BF)
        for part in normed
    ]
    emb = jnp.concatenate(emb, axis=0)
    copies = []
    for t in range(2):
        span = slice(t * 512, (t + 1) * 512)
        rows = jnp.dot(place[span], emb, preferred_element_type=F32)
        out[span, :] = jnp.where(taken[span] > 0, rows, EMPTY).astype(BF)
        part = pl.ds(t * 512, 512)
        copies += started([pltpu.make_async_copy(out.at[part], out_hbm.at[part], sems.at[2 + t])])
    finish(copies)


def turn_kernel(weight_ref, out_ref):
    for i in range(6):
        cols = slice(i * 384, (i + 1) * 384)
        out_ref[cols, :] = weight_ref[:, cols].T


def qkv_kernel(
    off_ref,
    me_ref,
    slots_ref,
    gain_ref,
    weight_hbm,
    q0_ref,
    kv0_ref,
    sa_hbm,
    sb_hbm,
    sc_hbm,
    sd_hbm,
    kv0_hbm,
    q0_hbm,
    wide,
    mixed,
    weight,
    sent,
    sems,
):
    loads = started([pltpu.make_async_copy(weight_hbm, weight, sems.at[0])])
    for c in range(D // 128):
        wide[c] = slots_ref[:, c * 128 : (c + 1) * 128].astype(F32)
    gain = row_of(gain_ref)

    def prepared(block):
        flags, normed = [], []
        for r in (2 * block, 2 * block + 1):
            rows = jnp.concatenate(
                [wide[c, pl.ds(r, OWNERS, stride=CAP), :] for c in range(D // 128)], axis=1
            )
            held = rows[:, :1] < LIMIT
            flags.append(jnp.broadcast_to(held.astype(F32), (OWNERS, 128)).T[:1])
            centred, scale = normalise(jnp.where(held, rows, 0.0))
            normed.append((centred * scale * gain).astype(BF))
        return jnp.concatenate(flags, axis=1) > 0, jnp.concatenate(normed, axis=0)

    state = prepared(0)
    finish(loads)
    for block in range(4):
        held, normed = state
        if block < 3:
            state = prepared(block + 1)
        lanes = slice(block * 256, (block + 1) * 256)
        for part in range(3):
            rows = slice(part * D, (part + 1) * D)
            made = lax.dot_general(weight[rows, :], normed, NT, preferred_element_type=F32)
            if part == 0:
                made = made * SCALE
            if part == 1:
                made = jnp.where(held, made, EMPTY)
            mixed[rows, lanes] = made.astype(BF)
    copies = started(
        [
            pltpu.make_async_copy(mixed.at[pl.ds(D, 4 * HD)], kv0_hbm.at[pl.ds(0, 4 * HD)], sems.at[1]),
            pltpu.make_async_copy(
                mixed.at[pl.ds(2 * D, 4 * HD)], kv0_hbm.at[pl.ds(4 * HD, 4 * HD)], sems.at[2]
            ),
            pltpu.make_async_copy(mixed.at[pl.ds(0, 4 * HD)], q0_hbm, sems.at[6]),
        ]
    )

    def piece(part, head, rank):
        lanes = pl.ds(pl.multiple_of(rank * OWNERS, OWNERS), OWNERS)
        return mixed[pl.ds(pl.multiple_of(part * D + head * HD, 16), HD), lanes]

    for m in (1, 2, 3, 0):
        ref = sent.at[m]
        place = lax.bitwise_xor(me_ref[0] % 4, m)
        for group, start, count in GROUPS:
            head = 4 * group + place
            for row, part in enumerate((1, 2, 0)):
                for i in range(count):
                    ref[row * HD : (row + 1) * HD, start + i * 128 : start + (i + 1) * 128] = piece(
                        part, head, off_ref[head] + 2**group * i
                    )
        target = (sa_hbm, sb_hbm, sc_hbm, sd_hbm)[m]
        copies += started([pltpu.make_async_copy(ref, target, sems.at[3 + m if m < 3 else 7])])
    q0_ref[...] = mixed[0 : 4 * HD, :]
    kv0_ref[0 : 4 * HD, :] = mixed[D : D + 4 * HD, :]
    kv0_ref[4 * HD :, :] = mixed[2 * D : 2 * D + 4 * HD, :]
    finish(copies)


def finish_keys(keys, values):
    width = keys.shape[1]
    top = iota((16, width), 0) == 0
    empty = keys[0:1, :].astype(F32) > LIMIT
    keys[HD:, :] = jnp.where(top & empty, MASKED, 0.0).astype(BF)
    keys[:HD, :] = jnp.where(empty, 0.0, keys[:HD, :].astype(F32)).astype(BF)
    values[HD:, :] = jnp.where(top, 1.0, 0.0).astype(BF)


def with_ones(query):
    width = query.shape[1]
    ones = jnp.where(iota((16, width), 0) == 0, 1.0, 0.0).astype(BF)
    return jnp.concatenate([query, ones], axis=0)


def attend(units):
    def score(unit):
        return jnp.dot(with_ones(unit[0]()).T, unit[1](), preferred_element_type=F32)

    scores = score(units[0])
    for i, unit in enumerate(units):
        top = jnp.max(scores, axis=1, keepdims=True)
        later = score(units[i + 1]) if i + 1 < len(units) else None
        weights = jnp.exp2(scores - top).astype(BF)
        sums = lax.dot_general(weights, unit[2](), NT, preferred_element_type=F32)
        unit[3](sums, top)
        scores = later


def divided(sums):
    turned = sums.T
    return (turned[:HD] / jnp.maximum(turned[HD : HD + 1], 1e-30)).astype(BF)


QT = 256


def units0(q_ref, keys, values, done):
    units = []
    for head in range(4):
        for t in range(SLOTS // QT):
            rows, lanes = slice(head * HD, (head + 1) * HD), slice(t * QT, (t + 1) * QT)
            units.append(
                (
                    lambda rows=rows, lanes=lanes: q_ref[rows, lanes],
                    lambda head=head: keys[head],
                    lambda head=head: values[head],
                    lambda sums, top, at=(head, rows, lanes): done(sums, top, *at),
                )
            )
    return units


def load0(kv_ref, keys, values):
    for head in range(4):
        keys[head, :HD] = kv_ref[head * HD : (head + 1) * HD, :]
        values[head, :HD] = kv_ref[(4 + head) * HD : (5 + head) * HD, :]
        finish_keys(keys.at[head], values.at[head])


def own_half_kernel(q_ref, kv_ref, out_hbm, keys, values, out, sems):
    copies = []
    load0(kv_ref, keys, values)

    def done(sums, top, head, rows, lanes):
        turned = jnp.where(iota((QT, 64), 1) == HD + 1, top, sums).T
        out[head, :, lanes] = turned
        if lanes.stop == SLOTS:
            copies.append(pltpu.make_async_copy(out.at[head], out_hbm.at[head], sems.at[head]))
            copies[-1].start()

    attend(units0(q_ref, keys, values, done))
    finish(copies)


def other_half_kernel(*refs):
    (q_ref, kv_ref, half_ref), sources = refs[:3], refs[3:7]
    out_ref, targets, (keys, values, sems) = refs[7], refs[8:12], refs[12:]
    copies = started(
        [
            pltpu.make_async_copy(source, target, sems.at[i])
            for i, (source, target) in enumerate(zip(sources, targets))
        ]
    )
    load0(kv_ref, keys, values)

    def done(sums, top, head, rows, lanes):
        mine = jnp.where(iota((QT, 64), 1) == HD + 1, top, sums).T
        before = half_ref[head, :, lanes]
        top_mine, top_before = mine[HD + 1 : HD + 2], before[HD + 1 : HD + 2]
        top = jnp.maximum(top_mine, top_before)
        total = mine * jnp.exp2(top_mine - top) + before * jnp.exp2(top_before - top)
        out_ref[rows, lanes] = (total[:HD] / jnp.maximum(total[HD : HD + 1], 1e-30)).astype(BF)

    attend(units0(q_ref, keys, values, done))
    finish(copies)


def pack_kernel(*refs):
    got, (far_hbm, farther_hbm, far, sems) = refs[:4], refs[4:]
    for s in range(4):
        far[:, s * 256 : (s + 1) * 256] = got[s][: 2 * HD, 512:768]
        far[:, 1024 + s * 128 : 1024 + (s + 1) * 128] = got[s][: 2 * HD, 768:]
    finish(
        started(
            [
                pltpu.make_async_copy(far, far_hbm, sems.at[0]),
                pltpu.make_async_copy(far.at[:, pl.ds(1024, 512)], farther_hbm, sems.at[1]),
            ]
        )
    )


def loader(keys, values):
    def load(at, block):
        width = block.shape[1]
        keys[:HD, at : at + width] = block[:HD]
        values[:HD, at : at + width] = block[HD:]

    return load


def joined_unit(got, outs, keys, values, parts):
    def query():
        blocks = [got[s][2 * HD :, lanes] for s, lanes in parts]
        return blocks[0] if len(blocks) == 1 else jnp.concatenate(blocks, axis=1)

    def done(sums, top):
        result, at = divided(sums), 0
        for s, lanes in parts:
            width = lanes.stop - lanes.start
            outs[s][:, lanes] = result[:, at : at + width]
            at += width

    return (query, lambda: keys[...], lambda: values[...], done)


def attend1_kernel(*refs):
    got, outs, (keys, values) = refs[:4], refs[4:8], refs[8:]
    load = loader(keys, values)
    for s in range(4):
        load(s * 512, got[s][: 2 * HD, :512])
    finish_keys(keys, values)
    attend(
        [
            joined_unit(got, outs, keys, values, [(s, slice(t * QT, (t + 1) * QT))])
            for s in range(4)
            for t in range(512 // QT)
        ]
    )


def attend23_kernel(*refs):
    got, (x4, x8, x12), first = refs[:4], refs[4:7], refs[7:11]
    outs, (keys, values, sent, sems) = refs[11:15], refs[15:]
    two, three = (keys.at[0], values.at[0]), (keys.at[1], values.at[1])
    for s in range(4):
        loader(*two)(s * 256, got[s][: 2 * HD, 512:768])
        loader(*three)(s * 128, got[s][: 2 * HD, 768:])
    loader(*two)(1024, x4[:, :1024])
    loader(*three)(512, x4[:, 1024:])
    loader(*three)(1024, x8[...])
    loader(*three)(1536, x12[...])
    finish_keys(*two)
    finish_keys(*three)
    made = [outs[0]] + [sent.at[m] for m in range(3)]
    for s in range(4):
        made[s][:, :512] = first[s][...]
    units = [joined_unit(got, made, *two, [(s, slice(512, 768))]) for s in range(4)]
    for s in (0, 2):
        lanes = slice(768, 896)
        units.append(joined_unit(got, made, *three, [(s, lanes), (s + 1, lanes)]))
    attend(units)
    finish(
        started([pltpu.make_async_copy(made[m], outs[m], sems.at[m - 1]) for m in range(1, 4)])
    )


def mlp_kernel(
    off_ref,
    me_ref,
    slots,
    a0_ref,
    aa_ref,
    ab_ref,
    ac_ref,
    ad_ref,
    gain_ref,
    out_weight,
    up,
    down,
    out_hbm,
    attn,
    wide,
    out,
    out_sems,
):
    part = 768
    parts = FF // part
    attn[: 4 * HD, :] = a0_ref[...]
    attn[4 * HD :, :] = jnp.zeros((12 * HD, SLOTS), BF)

    def lanes(rank):
        return pl.ds(pl.multiple_of(rank * OWNERS, OWNERS), OWNERS)

    for m, ref in enumerate((aa_ref, ab_ref, ac_ref, ad_ref)):
        place = lax.bitwise_xor(me_ref[0] % 4, m)
        for group, start, count in GROUPS:
            head = 4 * group + place
            rows = pl.ds(pl.multiple_of(head * HD, 16), HD)
            for i in range(count):
                attn[rows, lanes(off_ref[head] + 2**group * i)] = ref[
                    :, start + i * 128 : start + (i + 1) * 128
                ]

    for t in range(4):
        mixed = lax.dot_general(
            attn[:, t * 256 : (t + 1) * 256], out_weight[...], TN, preferred_element_type=F32
        )
        for i in range(2):
            for c in range(D // 128):
                wide[c, pl.ds(2 * t + i, OWNERS, stride=CAP), :] = mixed[
                    i * OWNERS : (i + 1) * OWNERS, c * 128 : (c + 1) * 128
                ]
    gain = row_of(gain_ref)
    tile = 512

    def written(t):
        span = pl.ds(pl.multiple_of(t * tile, tile), tile)
        return pltpu.make_async_copy(out.at[span], out_hbm.at[0, span], out_sems.at[t])

    def step(t, carry):
        span = pl.ds(pl.multiple_of(t * tile, tile), tile)
        rows = slots[span, :].astype(F32)
        held = rows[:, :1] < LIMIT
        mixed = jnp.concatenate([wide[c, span, :] for c in range(D // 128)], axis=1)
        hidden = jnp.where(held, rows, 0.0) + mixed
        centred, scale = normalise(hidden)
        normed = (centred * scale * gain).astype(BF)

        def raised(f):
            return jnp.dot(normed, up[:, f * part : (f + 1) * part], preferred_element_type=F32)

        final, act = hidden, raised(0)
        for f in range(parts):
            following = raised(f + 1) if f + 1 < parts else None
            final = final + jnp.dot(
                jax.nn.gelu(act).astype(BF),
                down[f * part : (f + 1) * part, :],
                preferred_element_type=F32,
            )
            act = following
        out[span, :] = jnp.where(held, final, 0.0).astype(BF)
        written(t).start()
        return carry

    lax.fori_loop(0, SLOTS // tile, step, 0)
    finish([written(t) for t in range(SLOTS // tile)])


def grad_kernel(
    dest_ref, feats_hbm, gain_ref, weight_hbm, back_hbm, out_hbm, feats, weight, back, out, sems
):
    loads = started(
        [
            pltpu.make_async_copy(back_hbm, back, sems.at[6]),
            pltpu.make_async_copy(weight_hbm, weight, sems.at[0]),
            pltpu.make_async_copy(feats_hbm, feats, sems.at[1]),
        ]
    )
    dest = dest_ref[...]
    slot = (dest * CAP + rank_of(dest)).astype(F32)
    slot = jnp.broadcast_to(slot, (128, TILES)).T[:, :1].astype(jnp.int32)
    gain = row_of(gain_ref)
    copies = []
    for t in range(2):
        span = slice(t * 256, (t + 1) * 256)
        place = (iota((256, SLOTS), 1) == slot[span]).astype(F32).astype(BF)
        if t == 0:
            loads[0].wait()
        rows = jnp.dot(place, back[...], preferred_element_type=F32).astype(BF)
        if t == 0:
            loads[1].wait()
        grad = lax.dot_general(rows, weight[...], NT, preferred_element_type=F32) * gain
        if t == 0:
            loads[2].wait()
        centred, scale = normalise(feats[span, :].astype(F32))
        unit = centred * scale
        along = jnp.mean(grad * unit, axis=-1, keepdims=True)
        level = jnp.mean(grad, axis=-1, keepdims=True)
        out[span, :] = (scale * (grad - level - unit * along)).astype(BF)
        part = pl.ds(t * 256, 256)
        copies += started([pltpu.make_async_copy(out.at[part], out_hbm.at[part], sems.at[2 + t])])
    finish(copies)


def per_device(
    tile_feats,
    tile_gain,
    proj_weight,
    proj_bias,
    dest,
    slot_gain,
    qkv_weight,
    out_weight,
    mlp_gain,
    up_weight,
    down_weight,
    offsets,
    slot_grad,
):
    sds = jax.ShapeDtypeStruct

    def in_hbm(array):
        return pltpu.with_memory_space_constraint(array, pltpu.HBM)

    def in_vmem(array):
        return pltpu.with_memory_space_constraint(array, pltpu.VMEM)

    everyone = ("tile", "seq")
    me = lax.axis_index("seq").astype(jnp.int32).reshape(1)
    dest = dest.reshape(1, TILES)
    order = lax.optimization_barrier

    outgoing = call(
        embed_kernel,
        sds((SLOTS, D), BF),
        (pltpu.VMEM((TILES, DT), BF), pltpu.VMEM((DT, D), BF), pltpu.VMEM((SLOTS, D), BF), DMA((4,))),
        VMEM,
        2 * 10**9,
        "embed_tiles",
        [VM, HBM, VM, HBM, VM],
        HBM,
    )(
        in_hbm(dest),
        in_hbm(tile_feats),
        in_hbm(tile_gain),
        in_hbm(proj_weight),
        in_hbm(proj_bias),
    )
    outgoing, qkv_weight = order((outgoing, qkv_weight))
    slots = lax.all_to_all(outgoing, everyone, split_axis=0, concat_axis=0, tiled=True)
    turned = call(turn_kernel, sds((3 * D, D), BF), (), VMEM, 8 * 10**9, "turn_qkv_weight")(
        qkv_weight
    )
    slots, turned, slot_grad = order((slots, turned, slot_grad))
    turned = in_hbm(turned)
    returned = lax.all_to_all(slot_grad[0], everyone, split_axis=0, concat_axis=0, tiled=True)

    part = sds((3 * HD, TAKEN), BF)
    kv0_shape = sds((8 * HD, SLOTS), BF)
    q0, kv0, *parts, kv0_sent, q0_kept = call(
        qkv_kernel,
        (
            sds((4 * HD, SLOTS), BF),
            kv0_shape,
            pltpu.HBM((3 * HD, TAKEN), BF),
            part,
            part,
            part,
            kv0_shape,
            pltpu.HBM((4 * HD, SLOTS), BF),
        ),
        (
            pltpu.VMEM((D // 128, SLOTS, 128), F32),
            pltpu.VMEM((3 * D, SLOTS), BF),
            pltpu.VMEM((3 * D, D), BF),
            pltpu.VMEM((4, 3 * HD, TAKEN), BF),
            DMA((8,)),
        ),
        VMEM,
        4 * 10**9,
        "make_qkv",
        [SM, SM, VM, VM, HBM],
        (VM, VM) + (HBM,) * 6,
    )(offsets, me, slots, in_hbm(slot_gain), turned)

    def send(array, m):
        return lax.ppermute(array, "seq", [(i, i ^ m) for i in range(N_SEQ)])

    one_head = (pltpu.VMEM((64, KEYS), BF), pltpu.VMEM((64, KEYS), BF))
    two_heads = (pltpu.VMEM((2, 64, KEYS), BF), pltpu.VMEM((2, 64, KEYS), BF))
    four_heads = (pltpu.VMEM((4, 64, SLOTS), BF), pltpu.VMEM((4, 64, SLOTS), BF))
    parts = [parts[0]] + [send(parts[m], m) for m in range(1, 4)]
    other = send(kv0_sent, 1)
    half = call(
        own_half_kernel,
        pltpu.HBM((4, 64, SLOTS), F32),
        four_heads + (pltpu.VMEM((4, 64, SLOTS), F32), DMA((4,))),
        VMEM,
        8 * 10**9,
        "attend_own_half",
        [VM, VM],
        HBM,
    )(q0, kv0)
    returned, half = order((returned, half))
    tile_grad = call(
        grad_kernel,
        sds((TILES, DT), BF),
        (
            pltpu.VMEM((TILES, DT), BF),
            pltpu.VMEM((DT, D), BF),
            pltpu.VMEM((SLOTS, D), BF),
            pltpu.VMEM((TILES, DT), BF),
            DMA((7,)),
        ),
        VMEM,
        4 * 10**9,
        "tile_cotangent",
        [VM, HBM, VM, HBM, HBM],
        HBM,
    )(
        in_hbm(dest),
        in_hbm(tile_feats),
        in_hbm(tile_gain),
        in_hbm(proj_weight),
        in_hbm(returned),
    )
    tile_grad, half, *parts = order((tile_grad, half, *parts))
    parts = [in_vmem(array) for array in parts]
    far, farther = call(
        pack_kernel,
        (sds((2 * HD, 1536), BF), sds((2 * HD, 512), BF)),
        (pltpu.VMEM((2 * HD, 1536), BF), DMA((2,))),
        VMEM,
        10**9,
        "pack_far_keys",
        None,
        (HBM, HBM),
    )(*parts)
    x12, x8, x4 = send(farther, 12), send(farther, 8), send(far, 4)
    result = sds((HD, TAKEN), BF)
    first = call(
        attend1_kernel, (sds((HD, 512), BF),) * 4, one_head, VMEM, 8 * 10**9, "attend_group1"
    )(*parts)
    x4, x8, x12, *first = order((x4, x8, x12, *first))
    rest = call(
        attend23_kernel,
        (result,) * 4,
        two_heads + (pltpu.VMEM((3, HD, TAKEN), BF), DMA((3,))),
        VMEM,
        6 * 10**9,
        "attend_groups23",
        None,
        (VM, HBM, HBM, HBM),
    )(*parts, x4, x8, x12, *first)
    other, half, *rest = order((other, half, *rest))
    rest = [rest[0]] + [send(rest[m], m) for m in range(1, 4)]
    a0, *held = call(
        other_half_kernel,
        (
            sds((4 * HD, SLOTS), BF),
            sds((SLOTS, D), BF),
            sds((D, D), BF),
            sds((D, FF), BF),
            sds((FF, D), BF),
        ),
        four_heads + (DMA((4,)),),
        VMEM,
        8 * 10**9,
        "attend_other_half",
        [VM] * 3 + [HBM] * 4,
    )(
        in_vmem(q0_kept),
        in_vmem(other),
        in_vmem(half),
        *(in_hbm(array) for array in (slots, out_weight, up_weight, down_weight)),
    )
    a0, *rest = order((a0, *rest))
    slots, out_weight, up_weight, down_weight = (in_vmem(array) for array in held)

    slide_states = call(
        mlp_kernel,
        sds((1, SLOTS, D), BF),
        (
            pltpu.VMEM((D, SLOTS), BF),
            pltpu.VMEM((D // 128, SLOTS, 128), F32),
            pltpu.VMEM((SLOTS, D), BF),
            DMA((2,)),
        ),
        40,
        11 * 10**9,
        "out_and_mlp",
        [SM, SM] + [VM] * 10,
        HBM,
    )(offsets, me, slots, a0, *rest, in_hbm(mlp_gain), out_weight, up_weight, down_weight)
    return (slide_states, tile_grad)


def solution(mesh):
    return jax.shard_map(
        per_device,
        mesh=mesh,
        in_specs=(
            P(("tile", "seq"), None),
            P(),
            P(),
            P(),
            P(("tile", "seq"), None),
            P(),
            P(),
            P(),
            P(),
            P(),
            P(),
            P(),
            P("tile", "seq", None),
        ),
        out_specs=(P("tile", "seq", None), P(("tile", "seq"), None)),
        check_vma=False,
    )
```
